512 devices in a mesh: gx: 32 (over x, z), gy: 16 (over y, core).
Axes of the slice: x: 4, y: 8, z: 8, core: 2. Of those that a mesh axis runs over, the one named last changes fastest.
Arguments:
- trajectory: float32 [4, 3, 2048, 2048], P(None, None, 'gx', 'gy'), may hold values from -4 to 4
- depth: float32 [2048, 2048], P('gx', 'gy'), may hold values from 1 to 4
- cotangent: float32 [3, 2048, 2048], P(None, 'gx', 'gy'), may hold values from -6 to 6
- line_inverse: float32 [2048, 2048], P('gx'), as said below
- column_inverse: float32 [2048, 2048], P('gy'), as said below
- gauge_owner: int32 [65536, 1], P(('gx', 'gy')), may hold values from 0 to 15; in each aligned block of 128 rows (0 to 127, 128 to 255, ...) at most 16 rows name the same one
- gauge_cell: int32 [65536], P(('gx', 'gy')), may hold values from 0 to 8191
- gauge_obs: float32 [4, 65536], P(None, ('gx', 'gy')), may hold values from -4 to 4
- gauge_weight: float32 [65536], P(('gx', 'gy')), may hold values from 0.5 to 2
Outputs:
- grad_state: float32 [3, 2048, 2048], P(None, 'gx', 'gy')
- grad_depth: float32 [2048, 2048], P('gx', 'gy')
- gauge_residual: float32 [4, 65536], P(None, ('gx', 'gy'))
The draws below stay inside these ranges and needn't reach their ends.
Inputs may be any that keep to these rules, and one draw needn't show every extreme that they name: `gauge_owner`: among the 128 gauges of one device no owner index appears more than 16 times, and some owner appears exactly 16 times. `line_inverse`: entries are positive. `column_inverse`: entries are positive.
All inputs are finite; a program needn't handle non-finite values.
Results may differ from the reference program's by a relative error of at most 0.00007.
Values sent between devices are 32-bit elements; how exact they have to be, the bound alone decides.
A program may use at most 64 MiB of HBM per device.

```python
import math
from functools import partial
import jax
import jax.numpy as jnp
import numpy as np
from jax import lax

CX = 64
CY = 128
STEPS = 4
GS = 128
NX = 2048
NY = 2048
CAP = 16
GAUGES = 65536
N_GY = 16


def banded_inverse(key, length):
    reach = 0.5 * length
    rows = jnp.arange(length, dtype=jnp.float32)[:, None]
    cols = jnp.arange(length, dtype=jnp.float32)[None, :]
    distance = jnp.abs(rows - cols)
    uniform_part = jax.random.uniform(key, (length, length), jnp.float32)
    factor = 0.02 + 1.96 * uniform_part
    spread = jnp.exp(-distance / reach) / length * factor
    return jnp.where(distance == 0.0, 0.1, 0.0) + spread


def draw_line_inverse(key, part):
    key = jax.random.fold_in(key, 11)
    return banded_inverse(key, NX)


def draw_column_inverse(key, part):
    key = jax.random.fold_in(key, 23)
    return banded_inverse(key, NY)


def draw_cotangent(key, part):
    key = jax.random.fold_in(key, 37)
    noise_key, wave_key, phase_key = jax.random.split(key, 3)
    rows = jnp.arange(NX, dtype=jnp.float32)[None, :, None] / NX
    cols = jnp.arange(NY, dtype=jnp.float32)[None, None, :] / NY
    waves = jax.random.randint(wave_key, (2, 3, 1, 1), 1, 3).astype(jnp.float32)
    phases = jax.random.uniform(phase_key, (2, 3, 1, 1), jnp.float32)
    smooth = jnp.cos(2.0 * math.pi * (waves[0] * rows + phases[0])) * jnp.cos(2.0 * math.pi * (waves[1] * cols + phases[1]))
    rough = jax.random.normal(noise_key, (3, NX, NY), jnp.float32)
    field = rough + 0.7 * smooth
    return jnp.clip(field, -6.0, 6.0)


def touch_ends(array, key, least, top_value):
    place = [jax.random.randint(jax.random.fold_in(key, axis), (), 0, length) for axis, length in enumerate(array.shape)]
    widest = array.shape.index(max(array.shape))
    neighbour = place[:widest] + [(place[widest] + 1) % array.shape[widest]] + place[widest + 1:]
    return array.at[tuple(place)].set(least).at[tuple(neighbour)].set(top_value)


def level_of(own_key, extent, pieces, smallest, largest):
    def one(position, blocks):
        heights = jax.random.uniform(jax.random.fold_in(jax.random.fold_in(own_key, 6), position), (blocks,), jnp.float32, smallest / len(pieces), largest / len(pieces))
        return jnp.repeat(jnp.exp(heights), extent[position] // blocks).reshape((-1,) + (1,) * (len(extent) - position - 1))

    gain = one(*pieces[0])
    for cut in pieces[1:]:
        gain = gain * one(*cut)
    return gain


def deal_out(key, own, number, rows, amount, top, most, skew):
    sequence = jax.random.permutation(key, amount)
    crowded, common = shares(amount, rows * top, most, skew, True), shares(amount, rows * top, most, skew, False)
    places = jnp.arange(amount)

    def named(tallies, turn):
        used = int((tallies > 0).sum())
        fixed = max(1, used // 4)
        passed = fixed + (places - fixed + turn * (used - fixed)) % max(1, amount - fixed)
        return jnp.zeros((amount,), jnp.int32).at[sequence[jnp.where(places < fixed, places, passed)]].set(jnp.asarray(tallies, jnp.int32))

    tallies = jnp.where(number % 4 == 0, named(crowded, number // 4), named(common, number - number // 4 - 1))
    mixed = jax.random.permutation(jax.random.fold_in(own, 3), amount)
    donor, receiver = mixed[0:amount // 2 * 2:2], mixed[1:amount // 2 * 2:2]
    room = jnp.minimum(tallies[donor] - 1, most - tallies[receiver]) // 2
    room = jnp.where((donor == sequence[0]) | (receiver == sequence[0]) | (tallies[receiver] == 0), 0, jnp.maximum(room, 0))
    passed = jax.random.randint(jax.random.fold_in(own, 4), (amount // 2,), 0, 1 << 20) % (room + 1)
    tallies = tallies.at[donor].add(-passed).at[receiver].add(passed)
    labels = jnp.searchsorted(jnp.cumsum(tallies), jnp.arange(rows * top), side="right").astype(jnp.int32)
    grid = labels.reshape(top, rows).T
    grid = grid[jax.random.permutation(jax.random.fold_in(own, 1), rows)]
    turn = jax.random.randint(jax.random.fold_in(own, 2), (rows, 1), 0, top)
    return jnp.take_along_axis(grid, (jnp.arange(top)[None, :] + turn) % top, axis=1)


def shares(count, total, bound, skew, full):
    weights = [(1 << 20) // math.isqrt(grade ** skew) + 1 for grade in range(1, count + 1)]
    largest = bound if full else min(bound, max(-(-total // count), total * weights[0] // sum(weights)))
    least = 1 if total - largest >= count - 1 else 0
    counts, spare = [largest] + [least] * (count - 1), total - largest - least * (count - 1)
    while spare > 0:
        candidates = [i for i in range(1, count) if counts[i] < largest] or [i for i in range(1, count) if counts[i] < bound]
        pool, budget = sum([weights[i] for i in candidates]), spare
        for i in candidates:
            more = min(bound - counts[i], max(1, budget * weights[i] // pool), spare)
            counts[i] = counts[i] + more
            spare = spare - more
    return np.array(counts)


def scatter_about(own_key, shape, width, most, pieces=(), held_as=jnp.bfloat16):
    entries = jax.random.normal(own_key, shape, jnp.float32) * width
    if len(pieces) > 0:
        entries = level_of(own_key, shape, pieces, -0.22, 0.18) * entries
    return jnp.clip(entries, min=-most, max=most).astype(held_as)


def setup_inputs(seed: int = 0) -> dict:
    splits = jax.random.split(jax.random.key(seed), 10)
    trajectory = scatter_about(splits[0], (STEPS, 3, NX, NY), 0.5, 4.0, ((2, 32), (3, 16)), jnp.float32)
    depth = jnp.clip(jnp.exp(math.log(4.0) - 1.3862944 * jax.random.uniform(splits[1], (NX, NY), jnp.float32) ** level_of(splits[1], (NX, NY), ((0, 32), (1, 16)), -0.2, 0.2)), 1.0, 4.0)
    cotangent = draw_cotangent(jax.random.fold_in(splits[9], 71), 0)
    line_inverse = draw_line_inverse(jax.random.fold_in(splits[9], 71), 0)
    column_inverse = draw_column_inverse(jax.random.fold_in(splits[9], 71), 0)
    gauge_owner_keys = jax.random.split(jax.random.fold_in(splits[5], 1), GAUGES // GS)
    gauge_owner_turns = jax.random.permutation(jax.random.fold_in(splits[5], 3), GAUGES // GS)
    gauge_owner = jax.vmap(lambda own, number: deal_out(jax.random.fold_in(splits[5], 2), own, number, GS, N_GY, 1, CAP, 2))(gauge_owner_keys, gauge_owner_turns).reshape((GAUGES, 1))
    gauge_cell = touch_ends(jax.random.randint(splits[6], (GAUGES,), 0, CX * CY), jax.random.fold_in(splits[6], 1), 0, (CX * CY) - 1).astype(jnp.int32)
    gauge_obs = scatter_about(splits[7], (STEPS, GAUGES), 0.5, 4.0, ((1, 512),), jnp.float32)
    gauge_weight = jnp.clip(jnp.exp(math.log(2.0) - 1.3862944 * jax.random.uniform(splits[8], (GAUGES,), jnp.float32) ** level_of(splits[8], (GAUGES,), ((0, 512),), -0.2, 0.2)), 0.5, 2.0)
    return {"trajectory": trajectory, "depth": depth, "cotangent": cotangent, "line_inverse": line_inverse, "column_inverse": column_inverse, "gauge_owner": gauge_owner, "gauge_cell": gauge_cell, "gauge_obs": gauge_obs, "gauge_weight": gauge_weight}


mass_rate = 0.25
slope_rate = 0.3
advect_rate = 0.2
highest = lax.Precision.HIGHEST

def gradient_along(field, axis):
    length = field.shape[axis]
    widths = [(0, 0)] * field.ndim
    widths[axis] = (2, 2)
    padded = jnp.pad(field, widths)

    def window(offset):
        return lax.slice_in_dim(padded, offset, offset + length, axis=axis)
    return (window(0) - 8.0 * window(1) + 8.0 * window(3) - window(4)) / 12.0

def advance(state, depth, line_inverse, column_inverse):
    surface, eastward, northward = (state[0], state[1], state[2])
    total = depth + surface
    new_surface = surface - mass_rate * (gradient_along(total * eastward, 0) + gradient_along(total * northward, 1))
    first = eastward - slope_rate * gradient_along(surface, 0) - advect_rate * (eastward * gradient_along(eastward, 0) + northward * gradient_along(eastward, 1))
    second = northward - slope_rate * gradient_along(surface, 1) - advect_rate * (eastward * gradient_along(northward, 0) + northward * gradient_along(northward, 1))
    new_east = jnp.matmul(line_inverse.T, first, precision=highest)
    new_north = jnp.matmul(second, column_inverse, precision=highest)
    return jnp.stack([new_surface, new_east, new_north])

def reference(trajectory, depth, cotangent, line_inverse, column_inverse, gauge_owner, gauge_cell, gauge_obs, gauge_weight):
    holder = jnp.arange(GAUGES, dtype=jnp.int32) // GS
    block = holder // N_GY
    owner = gauge_owner[:, 0]
    row_index = block * CX + gauge_cell // CY
    col_index = owner * CY + gauge_cell % CY
    gauge_residual = trajectory[:, 0][:, row_index, col_index] - gauge_obs
    adjoint = cotangent
    grad_depth = jnp.zeros(depth.shape, jnp.float32)
    model = partial(advance, line_inverse=line_inverse, column_inverse=column_inverse)
    for section in reversed(range(STEPS)):
        unused, pullback = jax.vjp(model, trajectory[section], depth)
        state_part, depth_part = pullback(adjoint)
        grad_depth = grad_depth + depth_part
        adjoint = state_part.at[0, row_index, col_index].add(gauge_weight * gauge_residual[section])
    return (adjoint, grad_depth, gauge_residual)
```

```python
import functools

import jax
import jax.numpy as jnp
from jax import lax
from jax.experimental import pallas as pl
from jax.experimental.pallas import tpu as pltpu
from jax.sharding import PartitionSpec as P

mass_rate = 0.25
slope_rate = 0.3
advect_rate = 0.2
MESH = pl.DeviceIdType.MESH
f32 = jnp.float32
bf16 = jnp.bfloat16

NX_CHIPS, NZ_CHIPS, NY_CHIPS = 4, 8, 8
NGX, NGY = 32, 16
STEPS, ROWS, COLS = 4, 64, 128
XS = (1, -1, 2)
RING = (1, -1, 2, -2, 3, -3, 4)


def wrap(value, count):
    return lax.rem(value + count, count)


def split2(value):
    high = value.astype(bf16)
    low = (value - high.astype(f32)).astype(bf16)
    return high, low


def split3(value):
    first = value.astype(bf16)
    rest = value - first.astype(f32)
    second = rest.astype(bf16)
    third = (rest - second.astype(f32)).astype(bf16)
    return first, second, third


def dot(a, b):
    return lax.dot_general(a, b, (((1,), (0,)), ((), ())), preferred_element_type=f32)


def dot_nt(a, b):
    return lax.dot_general(a, b, (((1,), (1,)), ((), ())), preferred_element_type=f32)


def iota(shape, dim):
    return lax.broadcasted_iota(jnp.int32, shape, dim)


def slope_x(field, rim):
    padded = jnp.concatenate([rim, field, rim], axis=0)
    count = padded.shape[0]

    def window(shift):
        return pltpu.roll(padded, shift, 0)[8 : 8 + ROWS]

    return (window(2) - window(count - 2) + 8.0 * (window(count - 1) - window(1))) * (1.0 / 12.0)


def slope_y(field, rim):
    lane = iota(field.shape, 1)
    outer = pltpu.roll(jnp.where(lane >= COLS - 2, rim, field), 2, 1) - pltpu.roll(
        jnp.where(lane < 2, rim, field), COLS - 2, 1
    )
    inner = pltpu.roll(jnp.where(lane < 1, rim, field), COLS - 1, 1) - pltpu.roll(
        jnp.where(lane >= COLS - 1, rim, field), 1, 1
    )
    return (outer + 8.0 * inner) * (1.0 / 12.0)


def kernel(
    traj_in,
    depth_in,
    cot_in,
    line_in,
    column_in,
    owner_in,
    cell_in,
    obs_in,
    weight_in,
    state_out,
    depth_out,
    residual_out,
    traj,
    depth,
    line,
    column,
    owner,
    cell,
    obs,
    weight,
    surf,
    ebuf,
    nbuf,
    eedge,
    nedge,
    xh_out,
    xh_in,
    yh_out,
    yh_in,
    lrim,
    crim,
    tx_in,
    ty_out,
    ty_in,
    gout,
    gin,
    rout,
    rin,
    onehot,
    ll,
    ct,
    cx,
    nn,
    ae,
    fields3,
    forcing,
    acc,
    base,
    coef,
    load_sem,
    e_send,
    e_zrecv,
    e_xrecv,
    n_send,
    n_yrecv,
    n_crecv,
    ee_send,
    ee_recv,
    ne_send,
    ne_recv,
    xh_send,
    xh_recv,
    yh_send,
    yh_recv,
    once_send,
    once_recv,
):
    gx = lax.axis_index("gx")
    gy = lax.axis_index("gy")
    x, z = lax.div(gx, NZ_CHIPS), lax.rem(gx, NZ_CHIPS)
    y, core = lax.div(gy, 2), lax.rem(gy, 2)
    nslot = core * NY_CHIPS + y

    def at_x(d):
        return (wrap(x + d, NX_CHIPS) * NZ_CHIPS + z, gy)

    def at_z(d):
        return (x * NZ_CHIPS + wrap(z + d, NZ_CHIPS), gy)

    def at_y(d):
        return (gx, wrap(y + d, NY_CHIPS) * 2 + core)

    sibling = (gx, y * 2 + 1 - core)
    above, below = (wrap(gx - 1, NGX), gy), (wrap(gx + 1, NGX), gy)
    before, after = (gx, wrap(gy - 1, NGY)), (gx, wrap(gy + 1, NGY))

    has_above = jnp.where(gx > 0, 1.0, 0.0).astype(f32)
    has_below = jnp.where(gx < NGX - 1, 1.0, 0.0).astype(f32)
    has_before = jnp.where(gy > 0, 1.0, 0.0).astype(f32)
    has_after = jnp.where(gy < NGY - 1, 1.0, 0.0).astype(f32)

    def merge_x(top, bottom):
        return jnp.where(iota(top.shape, 0) >= 4, top * has_above, bottom * has_below)

    def merge_y(left, right):
        return jnp.where(iota(left.shape, 0) >= 4, left * has_before, right * has_after)

    def send(src, dst, send_sem, recv_sem, device):
        pltpu.make_async_remote_copy(
            src_ref=src,
            dst_ref=dst,
            send_sem=send_sem,
            recv_sem=recv_sem,
            device_id=device,
            device_id_type=MESH,
        ).start()

    def arrive(ref, sem):
        pltpu.make_async_copy(ref, ref, sem).wait()

    loads = [
        pltpu.make_async_copy(src, dst, load_sem.at[i])
        for i, (src, dst) in enumerate(
            [
                (cot_in.at[0], surf),
                (cot_in.at[1], ebuf.at[0, gx]),
                (cot_in.at[2], nbuf.at[0, nslot]),
                (traj_in, traj),
                (depth_in, depth),
                (line_in, line),
                (column_in, column),
                (owner_in, owner),
                (cell_in, cell),
                (obs_in, obs),
                (weight_in, weight),
            ]
        )
    ]
    for copy in loads:
        copy.start()

    barrier = pltpu.get_barrier_semaphore()
    peers = (
        [at_x(d) for d in XS]
        + [at_z(d) for d in RING]
        + [(gx, lax.rem(gy + d, NGY)) for d in range(1, NGY)]
        + [above, below]
    )
    for peer in peers:
        pl.semaphore_signal(barrier, inc=1, device_id=peer, device_id_type=MESH)
    for copy in loads:
        copy.wait()
    pl.semaphore_wait(barrier, len(peers))

    def start_step(s):
        mine = ebuf.at[s, gx]
        for i, d in enumerate(RING):
            send(mine, mine, e_send, e_zrecv.at[s, i], at_z(d))
        own = nbuf.at[s, nslot]
        for i, d in enumerate(RING):
            send(own, own, n_send, n_yrecv.at[s, i], at_y(d))
        for j, d in enumerate(XS):
            send(mine, mine, e_send, e_xrecv.at[s, j], at_x(d))
        surface = surf[...]
        east = mine[...]
        north = own[...]
        xh_out[s, 0, 0] = surface[0:8]
        xh_out[s, 0, 1] = north[0:8]
        xh_out[s, 1, 0] = surface[ROWS - 8 :]
        xh_out[s, 1, 1] = north[ROWS - 8 :]
        send(xh_out.at[s, 0], xh_in.at[s, 1], xh_send, xh_recv.at[s, 1], above)
        send(xh_out.at[s, 1], xh_in.at[s, 0], xh_send, xh_recv.at[s, 0], below)
        turned = jnp.concatenate([surface, east], axis=0).T
        yh_out[s, 0] = turned[0:8]
        yh_out[s, 1] = turned[COLS - 8 :]
        send(yh_out.at[s, 0], yh_in.at[s, 1], yh_send, yh_recv.at[s, 1], before)
        send(yh_out.at[s, 1], yh_in.at[s, 0], yh_send, yh_recv.at[s, 0], after)
        send(own, own, n_send, n_crecv.at[s], sibling)

    def start_once():
        both = pl.ds(1, 2)
        send(traj.at[:, both, pl.ds(0, 8)], tx_in.at[1], once_send.at[0], once_recv.at[0], above)
        send(
            traj.at[:, both, pl.ds(ROWS - 8, 8)],
            tx_in.at[0],
            once_send.at[0],
            once_recv.at[1],
            below,
        )
        for t in range(STEPS):
            turned = jnp.concatenate([traj[t, 1], traj[t, 2]], axis=0).T
            ty_out[0, t] = turned[0:8]
            ty_out[1, t] = turned[COLS - 8 :]
        send(ty_out.at[0], ty_in.at[1], once_send.at[1], once_recv.at[2], before)
        send(ty_out.at[1], ty_in.at[0], once_send.at[1], once_recv.at[3], after)
        owners = owner[...]
        lane = iota((NGY, COLS), 1)
        member = jnp.where(iota((NGY, COLS), 0) == owners, 1.0, 0.0).astype(f32)
        upper = jnp.where(iota((COLS, COLS), 0) <= iota((COLS, COLS), 1), 1.0, 0.0).astype(bf16)
        counted = dot(member.astype(bf16), upper)
        rank = jnp.sum(counted * member, axis=0, keepdims=True).astype(jnp.int32) - 1
        target = owners * 16 + rank
        picked = jnp.where(iota((2 * COLS, COLS), 0) == target, 1.0, 0.0).astype(bf16)
        onehot[...] = picked
        cells = cell[...]
        row = lax.shift_right_logical(cells, 7).astype(f32)
        col = lax.bitwise_and(cells, COLS - 1).astype(f32)
        payload = jnp.concatenate([obs[...], weight[...], row, col, jnp.ones_like(row)], axis=0)
        placed = dot_nt(jnp.concatenate([p.astype(f32) for p in split3(payload)], axis=0).astype(bf16), picked)
        placed = placed[0:8] + placed[8:16] + placed[16:24]
        del lane
        mod = lax.rem(gy, 8)
        for d in range(NGY):
            half = placed[:, (d // 8) * COLS : (d // 8 + 1) * COLS]
            gout[d] = pltpu.roll(half, wrap(mod - d % 8, 8) * 16, 1)
        gin[gy] = gout[gy]
        for d in range(1, NGY):
            peer = lax.rem(gy + d, NGY)
            send(gout.at[peer], gin.at[gy], once_send.at[2], once_recv.at[4], (gx, peer))
        send(line.at[pl.ds(0, 8)], lrim.at[1], once_send.at[3], once_recv.at[5], above)
        send(line.at[pl.ds(ROWS - 8, 8)], lrim.at[0], once_send.at[3], once_recv.at[6], below)
        send(column.at[pl.ds(0, 8)], crim.at[1], once_send.at[4], once_recv.at[7], before)
        send(column.at[pl.ds(COLS - 8, 8)], crim.at[0], once_send.at[4], once_recv.at[8], after)

    def gauges():
        arrive(gin.at[pl.ds(0, NGY - 1)], once_recv.at[4])
        for t in range(STEPS):
            for p, piece in enumerate(split3(traj[t, 0])):
                fields3[pl.ds((p * STEPS + t) * ROWS, ROWS)] = piece
        mod = lax.rem(gy, 8)
        lane8 = iota((8, COLS), 1)
        total = None
        for half in range(2):
            record = gin[half * 8]
            for k in range(1, 8):
                record = jnp.where(lax.shift_right_logical(lane8, 4) == k, gin[half * 8 + k], record)
            valid = record[7:8] > 0.5
            row = record[5:6].astype(jnp.int32)
            col = record[6:7].astype(jnp.int32)
            in_col = jnp.where((iota((COLS, COLS), 0) == col) & valid, 1.0, 0.0).astype(bf16)
            in_row = jnp.where(iota((ROWS, COLS), 0) == row, 1.0, 0.0).astype(f32)
            seen = dot(fields3[...], in_col)
            misfits, parts = [], [[], [], []]
            for t in range(STEPS):
                at = [seen[(p * STEPS + t) * ROWS : (p * STEPS + t + 1) * ROWS] for p in range(3)]
                value = jnp.sum((at[0] + at[1] + at[2]) * in_row, axis=0, keepdims=True)
                misfit = jnp.where(valid, value - record[t : t + 1], 0.0)
                misfits.append(misfit)
                for p, piece in enumerate(split3(record[4:5] * misfit)):
                    parts[p].append((in_row * piece.astype(f32)).astype(bf16))
            back = jnp.concatenate(misfits + [jnp.zeros((4, COLS), f32)], axis=0)
            for k in range(8):
                rout[half * 8 + k] = pltpu.roll(back, wrap(mod - k, 8) * 16, 1)
            spread = dot_nt(jnp.concatenate(parts[0] + parts[1] + parts[2], axis=0), in_col)
            total = spread if total is None else total + spread
        size = STEPS * ROWS
        total = total[0:size] + total[size : 2 * size] + total[2 * size :]
        for t in range(STEPS):
            forcing[t] = total[t * ROWS : (t + 1) * ROWS]
        rin[gy] = rout[gy]
        for d in range(1, NGY):
            peer = lax.rem(gy + d, NGY)
            send(rout.at[peer], rin.at[gy], once_send.at[5], once_recv.at[9], (gx, peer))

    def prepare():
        arrive(lrim.at[0], once_recv.at[5])
        arrive(lrim.at[0], once_recv.at[6])
        arrive(crim.at[0], once_recv.at[7])
        arrive(crim.at[0], once_recv.at[8])
        high, low = split2(line[...])
        ll[pl.ds(0, ROWS)] = high
        ll[pl.ds(ROWS, ROWS)] = low
        rim = merge_x(lrim[0], lrim[1])
        high = rim.astype(bf16).astype(f32)
        ll[pl.ds(2 * ROWS, 16)] = jnp.concatenate([high, rim - high], axis=0).astype(bf16)
        rim = merge_y(crim[0], crim[1])
        high = rim.astype(bf16).astype(f32)
        cx[...] = jnp.concatenate([high, rim - high], axis=0).astype(bf16)
        for k in range(NGY):
            at = slice(k * COLS, (k + 1) * COLS)
            high, low = split2(column[:, at].T)
            ct[at, 0:COLS] = high
            ct[at, COLS : 2 * COLS] = low

    def rim_y(left, right):
        merged = merge_y(left, right)
        return jnp.concatenate([merged, jnp.zeros((COLS - 16, COLS), f32), merged], axis=0).T

    def step(s, carry):
        t = STEPS - 1 - s
        start_step(s)

        @pl.when(s == 0)
        def _():
            start_once()

        def from_z(i, d):
            block = ebuf.at[s, x * NZ_CHIPS + wrap(z - d, NZ_CHIPS)]
            arrive(block, e_zrecv.at[s, i])
            for j, a in enumerate(XS):
                send(block, block, e_send, e_xrecv.at[s, j], at_x(a))

        def from_y(i, d):
            block = nbuf.at[s, core * NY_CHIPS + wrap(y - d, NY_CHIPS)]
            arrive(block, n_yrecv.at[s, i])
            send(block, block, n_send, n_crecv.at[s], sibling)

        from_z(0, RING[0])
        from_z(1, RING[1])
        arrive(xh_in.at[s, 0], xh_recv.at[s, 0])
        arrive(xh_in.at[s, 1], xh_recv.at[s, 1])
        nedge[s, nslot] = merge_x(xh_in[s, 0, 1], xh_in[s, 1, 1])
        for d in RING:
            send(nedge.at[s, nslot], nedge.at[s, nslot], ne_send, ne_recv.at[s, 0], at_y(d))
        arrive(yh_in.at[s, 0], yh_recv.at[s, 0])
        arrive(yh_in.at[s, 0], yh_recv.at[s, 1])
        eedge[s, gx] = merge_y(yh_in[s, 0], yh_in[s, 1])
        for d in RING:
            send(eedge.at[s, gx], eedge.at[s, gx], ee_send, ee_recv.at[s, 0], at_z(d))
        from_y(0, RING[0])
        from_y(1, RING[1])
        from_z(2, RING[2])
        from_z(3, RING[3])

        @pl.when(s == 0)
        def _():
            arrive(tx_in.at[0], once_recv.at[0])
            arrive(tx_in.at[0], once_recv.at[1])
            arrive(ty_in.at[0], once_recv.at[2])
            arrive(ty_in.at[0], once_recv.at[3])

        surface = surf[...]
        east, north = traj[t, 1], traj[t, 2]
        whole = depth[...] + traj[t, 0]
        rim_surface = rim_y(yh_in[s, 0], yh_in[s, 1])[0:ROWS]
        flux_x = mass_rate * slope_x(surface, merge_x(xh_in[s, 0, 0], xh_in[s, 1, 0]))
        flux_y = mass_rate * slope_y(surface, rim_surface)
        gain = east * flux_x + north * flux_y
        depth_out[...] = jnp.where(s == 0, 0.0, depth_out[...]) + gain
        base[0] = surface + gain
        base[1] = whole * flux_x
        base[2] = whole * flux_y
        from_y(2, RING[2])
        from_y(3, RING[3])
        from_z(4, RING[4])
        from_z(5, RING[5])
        rims = rim_y(ty_in[0, t], ty_in[1, t])
        east_x = merge_x(tx_in[0, t, 0], tx_in[1, t, 0])
        north_x = merge_x(tx_in[0, t, 1], tx_in[1, t, 1])
        north_y = rims[ROWS:]
        coef[0] = 1.0 - advect_rate * slope_x(east, east_x)
        coef[1] = advect_rate * slope_x(north, north_x)
        coef[2] = advect_rate * slope_y(east, rims[0:ROWS])
        coef[3] = 1.0 - advect_rate * slope_y(north, north_y)
        from_z(6, RING[6])
        arrive(eedge.at[s, pl.ds(0, NZ_CHIPS - 1)], ee_recv.at[s, 0])
        line_edges = eedge.at[s, pl.ds(x * NZ_CHIPS, NZ_CHIPS)]
        for a in XS:
            send(line_edges, line_edges, ee_send, ee_recv.at[s, 1], at_x(a))
        from_y(4, RING[4])
        from_y(5, RING[5])
        from_y(6, RING[6])
        arrive(nedge.at[s, pl.ds(0, NY_CHIPS - 1)], ne_recv.at[s, 0])
        column_edges = nedge.at[s, pl.ds(core * NY_CHIPS, NY_CHIPS)]
        send(column_edges, column_edges, ne_send, ne_recv.at[s, 1], sibling)

        @pl.when(s == 0)
        def _():
            prepare()
            gauges()

        arrive(nbuf.at[s, pl.ds(0, NY_CHIPS)], n_crecv.at[s])
        arrive(nedge.at[s, pl.ds(0, NY_CHIPS)], ne_recv.at[s, 1])
        for k in range(NGY):
            at = ((k % NY_CHIPS) * 2 + k // NY_CHIPS) * COLS
            at = slice(at, at + COLS)
            high, low = split2(nbuf[s, k])
            nn[0:ROWS, at] = high
            nn[ROWS : 2 * ROWS, at] = low
            rim = nedge[s, k]
            high = rim.astype(bf16).astype(f32)
            nn[2 * ROWS : 2 * ROWS + 16, at] = jnp.concatenate([high, rim - high], axis=0).astype(bf16)
        product = dot(nn[...], ct[...])

        def joined(product):
            left, right = product[:, 0:COLS], product[:, COLS:]
            inner = left[0:ROWS] + (right[0:ROWS] + left[ROWS : 2 * ROWS])
            at = 2 * ROWS
            rim = left[at : at + 8] + (right[at : at + 8] + left[at + 8 : at + 16])
            return inner, rim

        def sides(product):
            rim = product[0:ROWS] + (pltpu.roll(product[0:ROWS], COLS - 8, 1) + product[ROWS : 2 * ROWS])
            return jnp.where(iota((ROWS, COLS), 1) < 8, rim, pltpu.roll(rim, COLS - 8, 1))

        def widened(product):
            return jnp.concatenate([product, jnp.zeros((2 * ROWS, COLS - 16), f32)], axis=1)

        column_adjoint, column_x = joined(product)
        column_y = sides(widened(dot_nt(nn[0 : 2 * ROWS, :], cx[...])))

        def line_part(at):
            blocks = ebuf[s, pl.ds(at * NZ_CHIPS, NZ_CHIPS)].reshape(NZ_CHIPS * ROWS, COLS)
            high, low = split2(blocks)
            lanes = pl.ds(pl.multiple_of(at * (NZ_CHIPS * ROWS), NZ_CHIPS * ROWS), NZ_CHIPS * ROWS)
            return dot(ll[:, lanes], jnp.concatenate([high, low], axis=1))

        acc[...] = line_part(x)
        for j in range(2):
            at = wrap(x - XS[j], NX_CHIPS)
            arrive(ebuf.at[s, pl.ds(0, NZ_CHIPS)], e_xrecv.at[s, j])
            acc[...] += line_part(at)
        arrive(eedge.at[s, pl.ds(0, 3 * NZ_CHIPS)], ee_recv.at[s, 1])
        lane = iota((8, COLS), 1)
        for k in range(NGX // 2):
            rim = jnp.where(lane < ROWS, pltpu.roll(eedge[s, 2 * k], ROWS, 1), eedge[s, 2 * k + 1])
            high = rim.astype(bf16).astype(f32)
            ae[:, k * COLS : (k + 1) * COLS] = jnp.concatenate([high, rim - high], axis=0).astype(bf16)
        line_y = sides(widened(dot_nt(ll[0 : 2 * ROWS, :], ae[...])))
        arrive(ebuf.at[s, pl.ds(0, NZ_CHIPS)], e_xrecv.at[s, 2])
        line_adjoint, line_x = joined(acc[...] + line_part(wrap(x - XS[2], NX_CHIPS)))

        along_x = slope_x(line_adjoint, line_x)
        along_y = slope_y(column_adjoint, column_y)
        surf[...] = base[0] + forcing[t] + slope_rate * (along_x + along_y)
        mixed = slope_x(east * line_adjoint, east_x * line_x) + slope_y(
            north * line_adjoint, north_y * line_y
        )
        ebuf[s + 1, gx] = (
            line_adjoint * coef[0] - column_adjoint * coef[1] + advect_rate * mixed + base[1]
        )
        mixed = slope_x(east * column_adjoint, east_x * column_x) + slope_y(
            north * column_adjoint, north_y * column_y
        )
        nbuf[s + 1, nslot] = (
            column_adjoint * coef[3] - line_adjoint * coef[2] + advect_rate * mixed + base[2]
        )

        arrive(ebuf.at[s, pl.ds(0, NGX - 1)], e_send)
        arrive(nbuf.at[s, pl.ds(0, NGY - 1)], n_send)
        arrive(eedge.at[s, pl.ds(0, NGX - 1)], ee_send)
        arrive(nedge.at[s, pl.ds(0, NGY - 1)], ne_send)
        arrive(xh_out.at[s], xh_send)
        arrive(yh_out.at[s], yh_send)
        return carry

    lax.fori_loop(0, STEPS, step, 0)

    state_out[0] = surf[...]
    state_out[1] = ebuf[STEPS, gx]
    state_out[2] = nbuf[STEPS, nslot]

    arrive(rin.at[pl.ds(0, NGY - 1)], once_recv.at[9])
    lane8 = iota((8, COLS), 1)
    halves = []
    for half in range(2):
        record = rin[half * 8]
        for k in range(1, 8):
            record = jnp.where(lax.shift_right_logical(lane8, 4) == k, rin[half * 8 + k], record)
        halves.append(record)
    returned = jnp.concatenate(halves, axis=1)
    pieces = jnp.concatenate([p.astype(f32) for p in split3(returned)], axis=0).astype(bf16)
    found = dot(pieces, onehot[...])
    residual_out[...] = found[0:4] + found[8:12] + found[16:20]
    arrive(tx_in, once_send.at[0])
    arrive(ty_out, once_send.at[1])
    arrive(gout.at[pl.ds(0, NGY - 1)], once_send.at[2])
    arrive(lrim, once_send.at[3])
    arrive(crim, once_send.at[4])
    arrive(rout.at[pl.ds(0, NGY - 1)], once_send.at[5])


def per_device(
    trajectory,
    depth,
    cotangent,
    line_inverse,
    column_inverse,
    gauge_owner,
    gauge_cell,
    gauge_obs,
    gauge_weight,
):
    vmem = pltpu.VMEM
    dma = pltpu.SemaphoreType.DMA
    scratch = [
        vmem((STEPS, 3, ROWS, COLS), f32),
        vmem((ROWS, COLS), f32),
        vmem((ROWS, 2048), f32),
        vmem((COLS, 2048), f32),
        vmem((1, COLS), jnp.int32),
        vmem((1, COLS), jnp.int32),
        vmem((STEPS, COLS), f32),
        vmem((1, COLS), f32),
        vmem((ROWS, COLS), f32),
        vmem((STEPS + 1, NGX, ROWS, COLS), f32),
        vmem((STEPS + 1, NGY, ROWS, COLS), f32),
        vmem((STEPS, NGX, 8, COLS), f32),
        vmem((STEPS, NGY, 8, COLS), f32),
        vmem((STEPS, 2, 2, 8, COLS), f32),
        vmem((STEPS, 2, 2, 8, COLS), f32),
        vmem((STEPS, 2, 8, COLS), f32),
        vmem((STEPS, 2, 8, COLS), f32),
        vmem((2, 8, 2048), f32),
        vmem((2, 8, 2048), f32),
        vmem((2, STEPS, 2, 8, COLS), f32),
        vmem((2, STEPS, 8, COLS), f32),
        vmem((2, STEPS, 8, COLS), f32),
        vmem((NGY, 8, COLS), f32),
        vmem((NGY, 8, COLS), f32),
        vmem((NGY, 8, COLS), f32),
        vmem((NGY, 8, COLS), f32),
        vmem((2 * COLS, COLS), bf16),
        vmem((2 * ROWS + 16, 2048), bf16),
        vmem((2048, 2 * COLS), bf16),
        vmem((16, 2048), bf16),
        vmem((2 * ROWS + 16, 2048), bf16),
        vmem((16, 2048), bf16),
        vmem((3 * STEPS * ROWS, COLS), bf16),
        vmem((STEPS, ROWS, COLS), f32),
        vmem((2 * ROWS + 16, 2 * COLS), f32),
        vmem((3, ROWS, COLS), f32),
        vmem((4, ROWS, COLS), f32),
        dma((11,)),
        dma,
        dma((STEPS, 7)),
        dma((STEPS, 3)),
        dma,
        dma((STEPS, 7)),
        dma((STEPS,)),
        dma,
        dma((STEPS, 2)),
        dma,
        dma((STEPS, 2)),
        dma,
        dma((STEPS, 2)),
        dma,
        dma((STEPS, 2)),
        dma((6,)),
        dma((10,)),
    ]
    anywhere = pl.BlockSpec(memory_space=pl.ANY)
    here = pl.BlockSpec(memory_space=pltpu.VMEM)
    return pl.pallas_call(
        kernel,
        name="adjoint",
        out_shape=(
            jax.ShapeDtypeStruct((3, ROWS, COLS), f32),
            jax.ShapeDtypeStruct((ROWS, COLS), f32),
            jax.ShapeDtypeStruct((STEPS, COLS), f32),
        ),
        in_specs=[anywhere] * 9,
        out_specs=(here, here, here),
        scratch_shapes=scratch,
        compiler_params=pltpu.CompilerParams(
            collective_id=0, has_side_effects=True, vmem_limit_bytes=48 * 2**20
        ),
    )(
        trajectory,
        depth,
        cotangent,
        line_inverse,
        column_inverse,
        gauge_owner.reshape(1, COLS),
        gauge_cell.reshape(1, COLS),
        gauge_obs,
        gauge_weight.reshape(1, COLS),
    )


def solution(mesh):
    return jax.shard_map(
        per_device,
        mesh=mesh,
        in_specs=(
            P(None, None, "gx", "gy"),
            P("gx", "gy"),
            P(None, "gx", "gy"),
            P("gx", None),
            P("gy", None),
            P(("gx", "gy"), None),
            P(("gx", "gy")),
            P(None, ("gx", "gy")),
            P(("gx", "gy")),
        ),
        out_specs=(P(None, "gx", "gy"), P("gx", "gy"), P(None, ("gx", "gy"))),
        check_vma=False,
    )
```

```python
import functools

import jax
import jax.numpy as jnp
from jax import lax
from jax.experimental import pallas as pl
from jax.experimental.pallas import tpu as pltpu
from jax.sharding import PartitionSpec as P

mass_rate = 0.25
slope_rate = 0.3
advect_rate = 0.2
MESH = pl.DeviceIdType.MESH
f32 = jnp.float32
bf16 = jnp.bfloat16

NX_CHIPS, NZ_CHIPS, NY_CHIPS = 4, 8, 8
NGX, NGY = 32, 16
STEPS, ROWS, COLS = 4, 64, 128
XS = (1, -1, 2)
RING = (1, -1, 2, -2, 3, -3, 4)


def wrap(value, count):
    return lax.rem(value + count, count)


def split2(value):
    high = value.astype(bf16)
    low = (value - high.astype(f32)).astype(bf16)
    return high, low


def split3(value):
    first = value.astype(bf16)
    rest = value - first.astype(f32)
    second = rest.astype(bf16)
    third = (rest - second.astype(f32)).astype(bf16)
    return first, second, third


def dot(a, b):
    return lax.dot_general(a, b, (((1,), (0,)), ((), ())), preferred_element_type=f32)


def dot_nt(a, b):
    return lax.dot_general(a, b, (((1,), (1,)), ((), ())), preferred_element_type=f32)


def iota(shape, dim):
    return lax.broadcasted_iota(jnp.int32, shape, dim)


def slope_x(field, rim):
    padded = jnp.concatenate([rim, field, rim], axis=0)
    count = padded.shape[0]

    def window(shift):
        return pltpu.roll(padded, shift, 0)[8 : 8 + ROWS]

    return (window(2) - window(count - 2) + 8.0 * (window(count - 1) - window(1))) * (1.0 / 12.0)


def slope_y(field, rim):
    lane = iota(field.shape, 1)
    outer = pltpu.roll(jnp.where(lane >= COLS - 2, rim, field), 2, 1) - pltpu.roll(
        jnp.where(lane < 2, rim, field), COLS - 2, 1
    )
    inner = pltpu.roll(jnp.where(lane < 1, rim, field), COLS - 1, 1) - pltpu.roll(
        jnp.where(lane >= COLS - 1, rim, field), 1, 1
    )
    return (outer + 8.0 * inner) * (1.0 / 12.0)


def kernel(
    traj_in,
    depth_in,
    cot_in,
    line_in,
    column_in,
    owner_in,
    cell_in,
    obs_in,
    weight_in,
    state_out,
    depth_out,
    residual_out,
    traj,
    depth,
    line,
    column,
    owner,
    cell,
    obs,
    weight,
    surf,
    ebuf,
    nbuf,
    eedge,
    nedge,
    xh_out,
    xh_in,
    yh_out,
    yh_in,
    lrim,
    crim,
    tx_in,
    ty_out,
    ty_in,
    gout,
    gin,
    rout,
    rin,
    lpart,
    lrimpart,
    lmerged,
    pout,
    pin,
    onehot,
    ll,
    ct,
    cx,
    nn,
    ae,
    ez,
    fields3,
    forcing,
    base,
    coef,
    load_sem,
    e_send,
    e_recv,
    p_send,
    p_recv,
    n_send,
    n_yrecv,
    n_crecv,
    ee_send,
    ee_recv,
    ne_send,
    ne_recv,
    xh_send,
    xh_recv,
    yh_send,
    yh_recv,
    l_send,
    l_recv,
    once_send,
    once_recv,
):
    gx = lax.axis_index("gx")
    gy = lax.axis_index("gy")
    x, z = lax.div(gx, NZ_CHIPS), lax.rem(gx, NZ_CHIPS)
    y, core = lax.div(gy, 2), lax.rem(gy, 2)
    nslot = core * NY_CHIPS + y

    def at_x(d):
        return (wrap(x + d, NX_CHIPS) * NZ_CHIPS + z, gy)

    def at_z(d):
        return (x * NZ_CHIPS + wrap(z + d, NZ_CHIPS), gy)

    def at_y(d):
        return (gx, wrap(y + d, NY_CHIPS) * 2 + core)

    sibling = (gx, y * 2 + 1 - core)
    above, below = (wrap(gx - 1, NGX), gy), (wrap(gx + 1, NGX), gy)
    before, after = (gx, wrap(gy - 1, NGY)), (gx, wrap(gy + 1, NGY))

    has_above = jnp.where(gx > 0, 1.0, 0.0).astype(f32)
    has_below = jnp.where(gx < NGX - 1, 1.0, 0.0).astype(f32)
    has_before = jnp.where(gy > 0, 1.0, 0.0).astype(f32)
    has_after = jnp.where(gy < NGY - 1, 1.0, 0.0).astype(f32)

    def merge_x(top, bottom):
        return jnp.where(iota(top.shape, 0) >= 4, top * has_above, bottom * has_below)

    def merge_y(left, right):
        return jnp.where(iota(left.shape, 0) >= 4, left * has_before, right * has_after)

    def send(src, dst, send_sem, recv_sem, device):
        pltpu.make_async_remote_copy(
            src_ref=src,
            dst_ref=dst,
            send_sem=send_sem,
            recv_sem=recv_sem,
            device_id=device,
            device_id_type=MESH,
        ).start()

    def arrive(ref, sem):
        pltpu.make_async_copy(ref, ref, sem).wait()

    loads = [
        pltpu.make_async_copy(src, dst, load_sem.at[i])
        for i, (src, dst) in enumerate(
            [
                (cot_in.at[0], surf),
                (cot_in.at[1], ebuf.at[0, z]),
                (cot_in.at[2], nbuf.at[0, nslot]),
                (traj_in, traj),
                (depth_in, depth),
                (line_in, line),
                (column_in, column),
                (owner_in, owner),
                (cell_in, cell),
                (obs_in, obs),
                (weight_in, weight),
            ]
        )
    ]
    for copy in loads:
        copy.start()

    barrier = pltpu.get_barrier_semaphore()
    peers = (
        [at_z(d) for d in reversed(RING)]
        + [(gx, lax.rem(gy + d, NGY)) for d in (8, 9, 7, 10, 6, 11, 5, 12, 4, 13, 3, 14, 2, 15, 1)]
        + [at_x(d) for d in reversed(XS)]
        + [above, below]
    )
    for peer in peers:
        pl.semaphore_signal(barrier, inc=1, device_id=peer, device_id_type=MESH)
    part = NZ_CHIPS * ROWS

    def part_of(at):
        return pl.ds(pl.multiple_of(at * part, part), part)

    def pack_gauges():
        owners = owner[...]
        member = jnp.where(iota((NGY, COLS), 0) == owners, 1.0, 0.0).astype(f32)
        upper = jnp.where(iota((COLS, COLS), 0) <= iota((COLS, COLS), 1), 1.0, 0.0).astype(bf16)
        counted = dot(member.astype(bf16), upper)
        rank = jnp.sum(counted * member, axis=0, keepdims=True).astype(jnp.int32) - 1
        target = owners * 16 + rank
        picked = jnp.where(iota((2 * COLS, COLS), 0) == target, 1.0, 0.0).astype(bf16)
        onehot[...] = picked
        cells = cell[...]
        row = lax.shift_right_logical(cells, 7).astype(f32)
        col = lax.bitwise_and(cells, COLS - 1).astype(f32)
        payload = jnp.concatenate([obs[...], weight[...], row, col, jnp.ones_like(row)], axis=0)
        parts = jnp.concatenate([p.astype(f32) for p in split3(payload)], axis=0).astype(bf16)
        placed = dot_nt(parts, picked)
        placed = placed[0:8] + placed[8:16] + placed[16:24]
        mod = lax.rem(gy, 8)
        for d in range(NGY):
            half = placed[:, (d // 8) * COLS : (d // 8 + 1) * COLS]
            gout[d] = pltpu.roll(half, wrap(mod - d % 8, 8) * 16, 1)

    def split_once():
        high, low = split2(line[:, part_of(x)])
        ll[0, 0:ROWS] = high
        ll[0, ROWS : 2 * ROWS] = low
        for k in range(NGY):
            at = slice(k * COLS, (k + 1) * COLS)
            high, low = split2(column[:, at].T)
            ct[at, 0:COLS] = high
            ct[at, COLS : 2 * COLS] = low
        for t in range(STEPS):
            for p, piece in enumerate(split3(traj[t, 0])):
                fields3[pl.ds((p * STEPS + t) * ROWS, ROWS)] = piece

    def send_z(s, these):
        mine = ebuf.at[s, z]
        for i in these:
            send(mine, mine, e_send.at[s], e_recv.at[s, i], at_z(RING[i]))

    def send_rims(s):
        surface = surf[...]
        turned = jnp.concatenate([surface, ebuf[s, z]], axis=0).T
        yh_out[s, 0] = turned[0:8]
        yh_out[s, 1] = turned[COLS - 8 :]
        send(yh_out.at[s, 0], yh_in.at[s, 1], yh_send.at[s], yh_recv.at[s, 1], before)
        send(yh_out.at[s, 1], yh_in.at[s, 0], yh_send.at[s], yh_recv.at[s, 0], after)

    def send_x_rims(s):
        surface = surf[...]
        north = nbuf[s, nslot]
        xh_out[s, 0, 0] = surface[0:8]
        xh_out[s, 0, 1] = north[0:8]
        xh_out[s, 1, 0] = surface[ROWS - 8 :]
        xh_out[s, 1, 1] = north[ROWS - 8 :]
        send(xh_out.at[s, 0], xh_in.at[s, 1], xh_send.at[s], xh_recv.at[s, 1], above)
        send(xh_out.at[s, 1], xh_in.at[s, 0], xh_send.at[s], xh_recv.at[s, 0], below)

    def send_y(s):
        own = nbuf.at[s, nslot]
        for i in (6, 5, 4, 3, 2, 1, 0):
            send(own, own, n_send.at[s], n_yrecv.at[s, i], at_y(RING[i]))
        send(own, own, n_send.at[s], n_crecv.at[s], sibling)

    def start_once():
        loads[5].wait()
        for j, d in enumerate(XS):
            piece = line.at[:, part_of(wrap(x + d, NX_CHIPS))]
            send(piece, lpart.at[j], l_send.at[0], l_recv.at[0, j], at_x(d))
        send(line.at[pl.ds(0, 8)], lrim.at[1], once_send.at[3], once_recv.at[5], above)
        send(line.at[pl.ds(ROWS - 8, 8)], lrim.at[0], once_send.at[3], once_recv.at[6], below)
        for i in (3, 4, 6, 7, 8, 9, 10):
            loads[i].wait()
        send(column.at[pl.ds(0, 8)], crim.at[1], once_send.at[4], once_recv.at[7], before)
        send(column.at[pl.ds(COLS - 8, 8)], crim.at[0], once_send.at[4], once_recv.at[8], after)
        pack_gauges()
        gin[gy] = gout[gy]
        for d in range(1, NGY):
            peer = lax.rem(gy + d, NGY)
            send(gout.at[peer], gin.at[gy], once_send.at[2], once_recv.at[4], (gx, peer))
        both = pl.ds(1, 2)
        send(traj.at[:, both, pl.ds(0, 8)], tx_in.at[1], once_send.at[0], once_recv.at[0], above)
        send(
            traj.at[:, both, pl.ds(ROWS - 8, 8)],
            tx_in.at[0],
            once_send.at[0],
            once_recv.at[1],
            below,
        )
        for t in range(STEPS):
            turned = jnp.concatenate([traj[t, 1], traj[t, 2]], axis=0).T
            ty_out[0, t] = turned[0:8]
            ty_out[1, t] = turned[COLS - 8 :]
        send(ty_out.at[0], ty_in.at[1], once_send.at[1], once_recv.at[2], before)
        send(ty_out.at[1], ty_in.at[0], once_send.at[1], once_recv.at[3], after)

    def gauges():
        arrive(gin.at[pl.ds(0, NGY - 1)], once_recv.at[4])
        mod = lax.rem(gy, 8)
        lane8 = iota((8, COLS), 1)
        total = None
        for half in range(2):
            record = gin[half * 8]
            for k in range(1, 8):
                record = jnp.where(lax.shift_right_logical(lane8, 4) == k, gin[half * 8 + k], record)
            valid = record[7:8] > 0.5
            row = record[5:6].astype(jnp.int32)
            col = record[6:7].astype(jnp.int32)
            in_col = jnp.where((iota((COLS, COLS), 0) == col) & valid, 1.0, 0.0).astype(bf16)
            in_row = jnp.where(iota((ROWS, COLS), 0) == row, 1.0, 0.0).astype(f32)
            seen = dot(fields3[...], in_col)
            misfits, parts = [], [[], [], []]
            for t in range(STEPS):
                at = [seen[(p * STEPS + t) * ROWS : (p * STEPS + t + 1) * ROWS] for p in range(3)]
                value = jnp.sum((at[0] + at[1] + at[2]) * in_row, axis=0, keepdims=True)
                misfit = jnp.where(valid, value - record[t : t + 1], 0.0)
                misfits.append(misfit)
                for p, piece in enumerate(split3(record[4:5] * misfit)):
                    parts[p].append((in_row * piece.astype(f32)).astype(bf16))
            back = jnp.concatenate(misfits + [jnp.zeros((4, COLS), f32)], axis=0)
            for k in range(8):
                rout[half * 8 + k] = pltpu.roll(back, wrap(mod - k, 8) * 16, 1)
            spread = dot_nt(jnp.concatenate(parts[0] + parts[1] + parts[2], axis=0), in_col)
            total = spread if total is None else total + spread
        size = STEPS * ROWS
        total = total[0:size] + total[size : 2 * size] + total[2 * size :]
        for t in range(STEPS):
            forcing[t] = total[t * ROWS : (t + 1) * ROWS]
        rin[gy] = rout[gy]
        for d in range(1, NGY):
            peer = lax.rem(gy + d, NGY)
            send(rout.at[peer], rin.at[gy], once_send.at[5], once_recv.at[9], (gx, peer))

    def pass_rims():
        arrive(lrim.at[0], once_recv.at[5])
        arrive(lrim.at[0], once_recv.at[6])
        lmerged[...] = merge_x(lrim[0], lrim[1])
        for j, d in enumerate(XS):
            piece = lmerged.at[:, part_of(wrap(x + d, NX_CHIPS))]
            send(piece, lrimpart.at[j], l_send.at[1], l_recv.at[1, j], at_x(d))

    def both_parts(rim):
        high = rim.astype(bf16).astype(f32)
        return jnp.concatenate([high, rim - high], axis=0).astype(bf16)

    def prepare():
        ll[0, 2 * ROWS :] = both_parts(lmerged[:, part_of(x)])
        for j in range(3):
            arrive(lpart.at[j], l_recv.at[0, j])
            high, low = split2(lpart[j])
            ll[1 + j, 0:ROWS] = high
            ll[1 + j, ROWS : 2 * ROWS] = low
            arrive(lrimpart.at[j], l_recv.at[1, j])
            ll[1 + j, 2 * ROWS :] = both_parts(lrimpart[j])

    def prepare_column():
        arrive(crim.at[0], once_recv.at[7])
        arrive(crim.at[0], once_recv.at[8])
        cx[...] = both_parts(merge_y(crim[0], crim[1]))

    def spread_y(merged):
        return jnp.concatenate([merged, jnp.zeros((COLS - 16, COLS), f32), merged], axis=0).T

    def rim_y(left, right):
        return spread_y(merge_y(left, right))

    def step(s, carry):
        t = STEPS - 1 - s
        def keep(at, block):
            high, low = split2(block)
            rows = pl.ds(pl.multiple_of(at * ROWS, ROWS), ROWS)
            ez[rows, 0:COLS] = high
            ez[rows, COLS : 2 * COLS] = low

        def from_z(i):
            at = wrap(z - RING[i], NZ_CHIPS)
            arrive(ebuf.at[s, at], e_recv.at[s, i])
            keep(at, ebuf[s, at])

        def from_y(i):
            block = nbuf.at[s, core * NY_CHIPS + wrap(y - RING[i], NY_CHIPS)]
            arrive(block, n_yrecv.at[s, i])
            send(block, block, n_send.at[s], n_crecv.at[s], sibling)

        keep(z, ebuf[s, z])
        arrive(yh_in.at[s, 0], yh_recv.at[s, 0])
        arrive(yh_in.at[s, 0], yh_recv.at[s, 1])
        eedge[s, z] = merge_y(yh_in[s, 0], yh_in[s, 1])
        for d in RING:
            send(eedge.at[s, z], eedge.at[s, z], ee_send.at[s], ee_recv.at[s], at_z(d))
        arrive(xh_in.at[s, 0], xh_recv.at[s, 0])
        arrive(xh_in.at[s, 1], xh_recv.at[s, 1])
        nedge[s, nslot] = merge_x(xh_in[s, 0, 1], xh_in[s, 1, 1])
        for d in RING:
            send(nedge.at[s, nslot], nedge.at[s, nslot], ne_send.at[s], ne_recv.at[s, 0], at_y(d))
        from_y(0)
        from_y(1)
        from_z(0)
        from_z(1)
        from_y(2)
        from_y(3)
        from_z(2)
        from_z(3)

        @pl.when(s == 0)
        def _():
            pass_rims()
            split_once()

        from_z(4)
        from_z(5)
        from_z(6)

        @pl.when(s == 0)
        def _():
            prepare()

        def line_share(slot):
            product = dot(ll[slot], ez[...])
            inner, rim = joined(product)
            return inner, rim, dot_nt(ae[...], ll[slot, 0 : 2 * ROWS, :])

        def joined(product):
            left, right = product[:, 0:COLS], product[:, COLS:]
            inner = left[0:ROWS] + (right[0:ROWS] + left[ROWS : 2 * ROWS])
            at = 2 * ROWS
            rim = left[at : at + 8] + (right[at : at + 8] + left[at + 8 : at + 16])
            return inner, rim

        def turned_rim(product):
            return product[0:8] + (pltpu.roll(product[0:8], ROWS, 1) + product[8:16])

        arrive(eedge.at[s, pl.ds(0, NZ_CHIPS - 1)], ee_recv.at[s])
        lane = iota((8, COLS), 1)
        for k in range(NZ_CHIPS // 2):
            rim = jnp.where(lane < ROWS, pltpu.roll(eedge[s, 2 * k], ROWS, 1), eedge[s, 2 * k + 1])
            ae[:, k * COLS : (k + 1) * COLS] = both_parts(rim)
        for j in (2, 0, 1):
            inner, rim, sides = line_share(1 + j)
            pout[s, j, 0:ROWS] = inner
            pout[s, j, ROWS : ROWS + 8] = rim
            pout[s, j, ROWS + 8 : ROWS + 16] = turned_rim(sides)
            send(pout.at[s, j], pin.at[s, j], p_send.at[s], p_recv.at[s, j], at_x(-XS[j]))
        from_y(4)
        from_y(5)
        from_y(6)
        arrive(nedge.at[s, pl.ds(0, NY_CHIPS - 1)], ne_recv.at[s, 0])
        column_edges = nedge.at[s, pl.ds(core * NY_CHIPS, NY_CHIPS)]
        send(column_edges, column_edges, ne_send.at[s], ne_recv.at[s, 1], sibling)
        line_adjoint, line_x, sides = line_share(0)
        line_y = turned_rim(sides)

        @pl.when(s == 0)
        def _():
            arrive(tx_in.at[0], once_recv.at[0])
            arrive(tx_in.at[0], once_recv.at[1])
            arrive(ty_in.at[0], once_recv.at[2])
            arrive(ty_in.at[0], once_recv.at[3])
            prepare_column()
            gauges()

        surface = surf[...]
        east, north = traj[t, 1], traj[t, 2]
        whole = depth[...] + traj[t, 0]
        rim_surface = rim_y(yh_in[s, 0], yh_in[s, 1])[0:ROWS]
        flux_x = mass_rate * slope_x(surface, merge_x(xh_in[s, 0, 0], xh_in[s, 1, 0]))
        flux_y = mass_rate * slope_y(surface, rim_surface)
        gain = east * flux_x + north * flux_y
        depth_out[...] = jnp.where(s == 0, 0.0, depth_out[...]) + gain
        base[0] = surface + gain
        base[1] = whole * flux_x
        base[2] = whole * flux_y
        rims = rim_y(ty_in[0, t], ty_in[1, t])
        east_x = merge_x(tx_in[0, t, 0], tx_in[1, t, 0])
        north_x = merge_x(tx_in[0, t, 1], tx_in[1, t, 1])
        north_y = rims[ROWS:]
        coef[0] = 1.0 - advect_rate * slope_x(east, east_x)
        coef[1] = advect_rate * slope_x(north, north_x)
        coef[2] = advect_rate * slope_y(east, rims[0:ROWS])
        coef[3] = 1.0 - advect_rate * slope_y(north, north_y)

        arrive(nbuf.at[s, pl.ds(0, NY_CHIPS)], n_crecv.at[s])
        arrive(nedge.at[s, pl.ds(0, NY_CHIPS)], ne_recv.at[s, 1])
        for k in range(NGY):
            at = ((k % NY_CHIPS) * 2 + k // NY_CHIPS) * COLS
            at = slice(at, at + COLS)
            high, low = split2(nbuf[s, k])
            nn[0:ROWS, at] = high
            nn[ROWS : 2 * ROWS, at] = low
            nn[2 * ROWS : 2 * ROWS + 16, at] = both_parts(nedge[s, k])
        column_adjoint, column_x = joined(dot(nn[...], ct[...]))
        column_y = spread_y(turned_rim(dot_nt(cx[...], nn[0 : 2 * ROWS, :])))[0:ROWS]

        for j in range(3):
            arrive(pin.at[s, j], p_recv.at[s, j])
            line_adjoint += pin[s, j, 0:ROWS]
            line_x += pin[s, j, ROWS : ROWS + 8]
            line_y += pin[s, j, ROWS + 8 : ROWS + 16]
        line_y = spread_y(line_y)[0:ROWS]

        along_x = slope_x(line_adjoint, line_x)
        along_y = slope_y(column_adjoint, column_y)
        mixed = slope_x(east * line_adjoint, east_x * line_x) + slope_y(
            north * line_adjoint, north_y * line_y
        )
        ebuf[s + 1, z] = (
            line_adjoint * coef[0] - column_adjoint * coef[1] + advect_rate * mixed + base[1]
        )

        surf[...] = base[0] + forcing[t] + slope_rate * (along_x + along_y)
        mixed = slope_x(east * column_adjoint, east_x * column_x) + slope_y(
            north * column_adjoint, north_y * column_y
        )
        nbuf[s + 1, nslot] = (
            column_adjoint * coef[3] - line_adjoint * coef[2] + advect_rate * mixed + base[2]
        )

        @pl.when(s < STEPS - 1)
        def _():
            send_rims(s + 1)
            send_x_rims(s + 1)
            send_z(s + 1, (6, 5, 4, 3, 2, 1, 0))
            send_y(s + 1)

        return carry

    for i in range(3):
        loads[i].wait()
    pl.semaphore_wait(barrier, len(peers))
    send_rims(0)
    send_x_rims(0)
    send_z(0, (6, 5, 4, 3, 2, 1, 0))
    send_y(0)
    start_once()
    lax.fori_loop(0, STEPS, step, 0)

    state_out[0] = surf[...]
    state_out[1] = ebuf[STEPS, z]
    state_out[2] = nbuf[STEPS, nslot]

    arrive(rin.at[pl.ds(0, NGY - 1)], once_recv.at[9])
    lane8 = iota((8, COLS), 1)
    halves = []
    for half in range(2):
        record = rin[half * 8]
        for k in range(1, 8):
            record = jnp.where(lax.shift_right_logical(lane8, 4) == k, rin[half * 8 + k], record)
        halves.append(record)
    returned = jnp.concatenate(halves, axis=1)
    pieces = jnp.concatenate([p.astype(f32) for p in split3(returned)], axis=0).astype(bf16)
    found = dot(pieces, onehot[...])
    residual_out[...] = found[0:4] + found[8:12] + found[16:20]
    for s in range(STEPS):
        arrive(ebuf.at[s, pl.ds(0, NZ_CHIPS - 1)], e_send.at[s])
        arrive(pout.at[s], p_send.at[s])
        arrive(nbuf.at[s, pl.ds(0, NGY - 1)], n_send.at[s])
        arrive(eedge.at[s, pl.ds(0, NZ_CHIPS - 1)], ee_send.at[s])
        arrive(nedge.at[s, pl.ds(0, NGY - 1)], ne_send.at[s])
        arrive(xh_out.at[s], xh_send.at[s])
        arrive(yh_out.at[s], yh_send.at[s])
    arrive(lpart, l_send.at[0])
    arrive(lrimpart, l_send.at[1])
    arrive(tx_in, once_send.at[0])
    arrive(ty_out, once_send.at[1])
    arrive(gout.at[pl.ds(0, NGY - 1)], once_send.at[2])
    arrive(lrim, once_send.at[3])
    arrive(crim, once_send.at[4])
    arrive(rout.at[pl.ds(0, NGY - 1)], once_send.at[5])


def hand_over(state_in, depth_in, residual_in, state_out, depth_out, residual_out):
    state_out[...] = state_in[...]
    depth_out[...] = depth_in[...]
    residual_out[...] = residual_in[...]


def per_device(
    trajectory,
    depth,
    cotangent,
    line_inverse,
    column_inverse,
    gauge_owner,
    gauge_cell,
    gauge_obs,
    gauge_weight,
):
    vmem = pltpu.VMEM
    dma = pltpu.SemaphoreType.DMA
    scratch = [
        vmem((STEPS, 3, ROWS, COLS), f32),
        vmem((ROWS, COLS), f32),
        vmem((ROWS, 2048), f32),
        vmem((COLS, 2048), f32),
        vmem((1, COLS), jnp.int32),
        vmem((1, COLS), jnp.int32),
        vmem((STEPS, COLS), f32),
        vmem((1, COLS), f32),
        vmem((ROWS, COLS), f32),
        vmem((STEPS + 1, NZ_CHIPS, ROWS, COLS), f32),
        vmem((STEPS + 1, NGY, ROWS, COLS), f32),
        vmem((STEPS, NZ_CHIPS, 8, COLS), f32),
        vmem((STEPS, NGY, 8, COLS), f32),
        vmem((STEPS, 2, 2, 8, COLS), f32),
        vmem((STEPS, 2, 2, 8, COLS), f32),
        vmem((STEPS, 2, 8, COLS), f32),
        vmem((STEPS, 2, 8, COLS), f32),
        vmem((2, 8, 2048), f32),
        vmem((2, 8, 2048), f32),
        vmem((2, STEPS, 2, 8, COLS), f32),
        vmem((2, STEPS, 8, COLS), f32),
        vmem((2, STEPS, 8, COLS), f32),
        vmem((NGY, 8, COLS), f32),
        vmem((NGY, 8, COLS), f32),
        vmem((NGY, 8, COLS), f32),
        vmem((NGY, 8, COLS), f32),
        vmem((3, ROWS, 512), f32),
        vmem((3, 8, 512), f32),
        vmem((8, 2048), f32),
        vmem((STEPS, 3, ROWS + 16, COLS), f32),
        vmem((STEPS, 3, ROWS + 16, COLS), f32),
        vmem((2 * COLS, COLS), bf16),
        vmem((4, 2 * ROWS + 16, 512), bf16),
        vmem((2048, 2 * COLS), bf16),
        vmem((16, 2048), bf16),
        vmem((2 * ROWS + 16, 2048), bf16),
        vmem((16, 512), bf16),
        vmem((512, 2 * COLS), bf16),
        vmem((3 * STEPS * ROWS, COLS), bf16),
        vmem((STEPS, ROWS, COLS), f32),
        vmem((3, ROWS, COLS), f32),
        vmem((4, ROWS, COLS), f32),
        dma((11,)),
        dma((STEPS,)),
        dma((STEPS, 7)),
        dma((STEPS,)),
        dma((STEPS, 3)),
        dma((STEPS,)),
        dma((STEPS, 7)),
        dma((STEPS,)),
        dma((STEPS,)),
        dma((STEPS,)),
        dma((STEPS,)),
        dma((STEPS, 2)),
        dma((STEPS,)),
        dma((STEPS, 2)),
        dma((STEPS,)),
        dma((STEPS, 2)),
        dma((2,)),
        dma((2, 3)),
        dma((6,)),
        dma((10,)),
    ]
    anywhere = pl.BlockSpec(memory_space=pl.ANY)
    here = pl.BlockSpec(memory_space=pltpu.VMEM)
    results = pl.pallas_call(
        kernel,
        name="adjoint",
        out_shape=(
            jax.ShapeDtypeStruct((3, ROWS, COLS), f32),
            jax.ShapeDtypeStruct((ROWS, COLS), f32),
            jax.ShapeDtypeStruct((STEPS, COLS), f32),
        ),
        in_specs=[anywhere] * 9,
        out_specs=(here, here, here),
        scratch_shapes=scratch,
        compiler_params=pltpu.CompilerParams(
            collective_id=0, has_side_effects=True, vmem_limit_bytes=60 * 2**20
        ),
    )(
        trajectory,
        depth,
        cotangent,
        line_inverse,
        column_inverse,
        gauge_owner.reshape(1, COLS),
        gauge_cell.reshape(1, COLS),
        gauge_obs,
        gauge_weight.reshape(1, COLS),
    )
    return pl.pallas_call(
        hand_over,
        name="hand_over",
        out_shape=tuple(jax.ShapeDtypeStruct(r.shape, r.dtype) for r in results),
        in_specs=[here] * 3,
        out_specs=(here, here, here),
    )(*results)


def solution(mesh):
    return jax.shard_map(
        per_device,
        mesh=mesh,
        in_specs=(
            P(None, None, "gx", "gy"),
            P("gx", "gy"),
            P(None, "gx", "gy"),
            P("gx", None),
            P("gy", None),
            P(("gx", "gy"), None),
            P(("gx", "gy")),
            P(None, ("gx", "gy")),
            P(("gx", "gy")),
        ),
        out_specs=(P(None, "gx", "gy"), P("gx", "gy"), P(None, ("gx", "gy"))),
        check_vma=False,
    )
```

```python
import functools

import jax
import jax.numpy as jnp
from jax import lax
from jax.experimental import pallas as pl
from jax.experimental.pallas import tpu as pltpu
from jax.sharding import PartitionSpec as P

mass_rate = 0.25
slope_rate = 0.3
advect_rate = 0.2
MESH = pl.DeviceIdType.MESH
f32 = jnp.float32
bf16 = jnp.bfloat16

NX_CHIPS, NZ_CHIPS, NY_CHIPS = 4, 8, 8
NGX, NGY = 32, 16
STEPS, ROWS, COLS = 4, 64, 128
XS = (1, -1, 2)
RING = (1, -1, 2, -2, 3, -3, 4)


def wrap(value, count):
    return lax.rem(value + count, count)


def split2(value):
    high = value.astype(bf16)
    low = (value - high.astype(f32)).astype(bf16)
    return high, low


def split3(value):
    first = value.astype(bf16)
    rest = value - first.astype(f32)
    second = rest.astype(bf16)
    third = (rest - second.astype(f32)).astype(bf16)
    return first, second, third


def dot(a, b):
    return lax.dot_general(a, b, (((1,), (0,)), ((), ())), preferred_element_type=f32)


def dot_nt(a, b):
    return lax.dot_general(a, b, (((1,), (1,)), ((), ())), preferred_element_type=f32)


def iota(shape, dim):
    return lax.broadcasted_iota(jnp.int32, shape, dim)


def slope_x(field, rim):
    padded = jnp.concatenate([rim, field, rim], axis=0)
    count = padded.shape[0]

    def window(shift):
        return pltpu.roll(padded, shift, 0)[8 : 8 + ROWS]

    return (window(2) - window(count - 2) + 8.0 * (window(count - 1) - window(1))) * (1.0 / 12.0)


def slope_y(field, rim):
    lane = iota(field.shape, 1)
    outer = pltpu.roll(jnp.where(lane >= COLS - 2, rim, field), 2, 1) - pltpu.roll(
        jnp.where(lane < 2, rim, field), COLS - 2, 1
    )
    inner = pltpu.roll(jnp.where(lane < 1, rim, field), COLS - 1, 1) - pltpu.roll(
        jnp.where(lane >= COLS - 1, rim, field), 1, 1
    )
    return (outer + 8.0 * inner) * (1.0 / 12.0)


def kernel(
    traj_in,
    depth_in,
    cot_in,
    line_in,
    column_in,
    owner_in,
    cell_in,
    obs_in,
    weight_in,
    state_out,
    depth_out,
    residual_out,
    traj,
    depth,
    line,
    column,
    owner,
    cell,
    obs,
    weight,
    surf,
    ebuf,
    nbuf,
    eedge,
    nedge,
    xh_out,
    xh_in,
    yh_out,
    yh_in,
    lrim,
    crim,
    tx_in,
    ty_out,
    ty_in,
    gout,
    gin,
    rout,
    rin,
    lpart,
    lrimpart,
    lmerged,
    pout,
    pin,
    qout,
    qin,
    onehot,
    ll,
    ct,
    cx,
    nn,
    ae,
    ez,
    fields3,
    forcing,
    base,
    coef,
    load_sem,
    e_send,
    e_recv,
    p_send,
    p_recv,
    q_send,
    q_recv,
    n_send,
    n_yrecv,
    n_crecv,
    ee_send,
    ee_recv,
    ne_send,
    ne_recv,
    xh_send,
    xh_recv,
    yh_send,
    yh_recv,
    l_send,
    l_recv,
    once_send,
    once_recv,
):
    gx = lax.axis_index("gx")
    gy = lax.axis_index("gy")
    x, z = lax.div(gx, NZ_CHIPS), lax.rem(gx, NZ_CHIPS)
    y, core = lax.div(gy, 2), lax.rem(gy, 2)
    nslot = core * NY_CHIPS + y

    def at_x(d):
        return (wrap(x + d, NX_CHIPS) * NZ_CHIPS + z, gy)

    def at_z(d):
        return (x * NZ_CHIPS + wrap(z + d, NZ_CHIPS), gy)

    def at_y(d):
        return (gx, wrap(y + d, NY_CHIPS) * 2 + core)

    sibling = (gx, y * 2 + 1 - core)
    above, below = (wrap(gx - 1, NGX), gy), (wrap(gx + 1, NGX), gy)
    before, after = (gx, wrap(gy - 1, NGY)), (gx, wrap(gy + 1, NGY))

    has_above = jnp.where(gx > 0, 1.0, 0.0).astype(f32)
    has_below = jnp.where(gx < NGX - 1, 1.0, 0.0).astype(f32)
    has_before = jnp.where(gy > 0, 1.0, 0.0).astype(f32)
    has_after = jnp.where(gy < NGY - 1, 1.0, 0.0).astype(f32)

    def merge_x(top, bottom):
        return jnp.where(iota(top.shape, 0) >= 4, top * has_above, bottom * has_below)

    def merge_y(left, right):
        return jnp.where(iota(left.shape, 0) >= 4, left * has_before, right * has_after)

    def send(src, dst, send_sem, recv_sem, device):
        pltpu.make_async_remote_copy(
            src_ref=src,
            dst_ref=dst,
            send_sem=send_sem,
            recv_sem=recv_sem,
            device_id=device,
            device_id_type=MESH,
        ).start()

    def arrive(ref, sem):
        pltpu.make_async_copy(ref, ref, sem).wait()

    loads = [
        pltpu.make_async_copy(src, dst, load_sem.at[i])
        for i, (src, dst) in enumerate(
            [
                (cot_in.at[0], surf),
                (cot_in.at[1], ebuf.at[0, z]),
                (cot_in.at[2], nbuf.at[0, nslot]),
                (traj_in, traj),
                (depth_in, depth),
                (line_in, line),
                (column_in, column),
                (owner_in, owner),
                (cell_in, cell),
                (obs_in, obs),
                (weight_in, weight),
            ]
        )
    ]

    barrier = pltpu.get_barrier_semaphore()
    peers = (
        [at_z(d) for d in reversed(RING)]
        + [(gx, lax.rem(gy + d, NGY)) for d in (8, 9, 7, 10, 6, 11, 5, 12, 4, 13, 3, 14, 2, 15, 1)]
        + [at_x(d) for d in reversed(XS)]
        + [above, below]
    )
    for peer in peers:
        pl.semaphore_signal(barrier, inc=1, device_id=peer, device_id_type=MESH)
    for copy in loads:
        copy.start()
    part = NZ_CHIPS * ROWS

    def part_of(at):
        return pl.ds(pl.multiple_of(at * part, part), part)

    def pack_gauges():
        owners = owner[...]
        member = jnp.where(iota((NGY, COLS), 0) == owners, 1.0, 0.0).astype(f32)
        upper = jnp.where(iota((COLS, COLS), 0) <= iota((COLS, COLS), 1), 1.0, 0.0).astype(bf16)
        counted = dot(member.astype(bf16), upper)
        rank = jnp.sum(counted * member, axis=0, keepdims=True).astype(jnp.int32) - 1
        target = owners * 16 + rank
        picked = jnp.where(iota((2 * COLS, COLS), 0) == target, 1.0, 0.0).astype(bf16)
        onehot[...] = picked
        cells = cell[...]
        row = lax.shift_right_logical(cells, 7).astype(f32)
        col = lax.bitwise_and(cells, COLS - 1).astype(f32)
        payload = jnp.concatenate([obs[...], weight[...], row, col, jnp.ones_like(row)], axis=0)
        parts = jnp.concatenate([p.astype(f32) for p in split3(payload)], axis=0).astype(bf16)
        placed = dot_nt(parts, picked)
        placed = placed[0:8] + placed[8:16] + placed[16:24]
        mod = lax.rem(gy, 8)
        for d in range(NGY):
            half = placed[:, (d // 8) * COLS : (d // 8 + 1) * COLS]
            gout[d] = pltpu.roll(half, wrap(mod - d % 8, 8) * 16, 1)

    def split_once():
        high, low = split2(line[:, part_of(x)])
        ll[0, 0:ROWS] = high
        ll[0, ROWS : 2 * ROWS] = low
        for k in range(NGY):
            at = slice(k * COLS, (k + 1) * COLS)
            high, low = split2(column[:, at].T)
            ct[at, 0:COLS] = high
            ct[at, COLS : 2 * COLS] = low
        for t in range(STEPS):
            for p, piece in enumerate(split3(traj[t, 0])):
                fields3[pl.ds((p * STEPS + t) * ROWS, ROWS)] = piece

    def send_z(s, these):
        mine = ebuf.at[s, z]
        for i in these:
            send(mine, mine, e_send.at[s], e_recv.at[s, i], at_z(RING[i]))

    def send_rims(s):
        surface = surf[...]
        turned = jnp.concatenate([surface, ebuf[s, z]], axis=0).T
        yh_out[s, 0] = turned[0:8]
        yh_out[s, 1] = turned[COLS - 8 :]
        send(yh_out.at[s, 0], yh_in.at[s, 1], yh_send.at[s], yh_recv.at[s, 1], before)
        send(yh_out.at[s, 1], yh_in.at[s, 0], yh_send.at[s], yh_recv.at[s, 0], after)

    def send_x_rims(s):
        surface = surf[...]
        north = nbuf[s, nslot]
        xh_out[s, 0, 0] = surface[0:8]
        xh_out[s, 0, 1] = north[0:8]
        xh_out[s, 1, 0] = surface[ROWS - 8 :]
        xh_out[s, 1, 1] = north[ROWS - 8 :]
        send(xh_out.at[s, 0], xh_in.at[s, 1], xh_send.at[s], xh_recv.at[s, 1], above)
        send(xh_out.at[s, 1], xh_in.at[s, 0], xh_send.at[s], xh_recv.at[s, 0], below)

    def send_y(s):
        own = nbuf.at[s, nslot]
        for i in (6, 5, 4, 3, 2, 1, 0):
            send(own, own, n_send.at[s], n_yrecv.at[s, i], at_y(RING[i]))
        send(own, own, n_send.at[s], n_crecv.at[s], sibling)

    def start_once():
        for j, d in enumerate(XS):
            piece = line.at[:, part_of(wrap(x + d, NX_CHIPS))]
            send(piece, lpart.at[j], l_send.at[0], l_recv.at[0, j], at_x(d))
        for i in (3, 4, 6, 7, 8, 9, 10):
            loads[i].wait()
        send(column.at[pl.ds(0, 8)], crim.at[1], once_send.at[4], once_recv.at[7], before)
        send(column.at[pl.ds(COLS - 8, 8)], crim.at[0], once_send.at[4], once_recv.at[8], after)
        pack_gauges()
        gin[gy] = gout[gy]
        for d in range(1, NGY):
            peer = lax.rem(gy + d, NGY)
            send(gout.at[peer], gin.at[gy], once_send.at[2], once_recv.at[4], (gx, peer))
        both = pl.ds(1, 2)
        send(traj.at[:, both, pl.ds(0, 8)], tx_in.at[1], once_send.at[0], once_recv.at[0], above)
        send(
            traj.at[:, both, pl.ds(ROWS - 8, 8)],
            tx_in.at[0],
            once_send.at[0],
            once_recv.at[1],
            below,
        )
        for t in range(STEPS):
            turned = jnp.concatenate([traj[t, 1], traj[t, 2]], axis=0).T
            ty_out[0, t] = turned[0:8]
            ty_out[1, t] = turned[COLS - 8 :]
        send(ty_out.at[0], ty_in.at[1], once_send.at[1], once_recv.at[2], before)
        send(ty_out.at[1], ty_in.at[0], once_send.at[1], once_recv.at[3], after)

    def gauges():
        arrive(gin.at[pl.ds(0, NGY - 1)], once_recv.at[4])
        mod = lax.rem(gy, 8)
        lane8 = iota((8, COLS), 1)
        total = None
        for half in range(2):
            record = gin[half * 8]
            for k in range(1, 8):
                record = jnp.where(lax.shift_right_logical(lane8, 4) == k, gin[half * 8 + k], record)
            valid = record[7:8] > 0.5
            row = record[5:6].astype(jnp.int32)
            col = record[6:7].astype(jnp.int32)
            in_col = jnp.where((iota((COLS, COLS), 0) == col) & valid, 1.0, 0.0).astype(bf16)
            in_row = jnp.where(iota((ROWS, COLS), 0) == row, 1.0, 0.0).astype(f32)
            seen = dot(fields3[...], in_col)
            misfits, parts = [], [[], [], []]
            for t in range(STEPS):
                at = [seen[(p * STEPS + t) * ROWS : (p * STEPS + t + 1) * ROWS] for p in range(3)]
                value = jnp.sum((at[0] + at[1] + at[2]) * in_row, axis=0, keepdims=True)
                misfit = jnp.where(valid, value - record[t : t + 1], 0.0)
                misfits.append(misfit)
                for p, piece in enumerate(split3(record[4:5] * misfit)):
                    parts[p].append((in_row * piece.astype(f32)).astype(bf16))
            back = jnp.concatenate(misfits + [jnp.zeros((4, COLS), f32)], axis=0)
            for k in range(8):
                rout[half * 8 + k] = pltpu.roll(back, wrap(mod - k, 8) * 16, 1)
            spread = dot_nt(jnp.concatenate(parts[0] + parts[1] + parts[2], axis=0), in_col)
            total = spread if total is None else total + spread
        size = STEPS * ROWS
        total = total[0:size] + total[size : 2 * size] + total[2 * size :]
        for t in range(STEPS):
            forcing[t] = total[t * ROWS : (t + 1) * ROWS]
        rin[gy] = rout[gy]
        for d in range(1, NGY):
            peer = lax.rem(gy + d, NGY)
            send(rout.at[peer], rin.at[gy], once_send.at[5], once_recv.at[9], (gx, peer))

    def pass_rims():
        arrive(lrim.at[0], once_recv.at[5])
        arrive(lrim.at[0], once_recv.at[6])
        lmerged[...] = merge_x(lrim[0], lrim[1])
        for j, d in enumerate(XS):
            piece = lmerged.at[:, part_of(wrap(x + d, NX_CHIPS))]
            send(piece, lrimpart.at[j], l_send.at[1], l_recv.at[1, j], at_x(d))

    def both_parts(rim):
        high = rim.astype(bf16).astype(f32)
        return jnp.concatenate([high, rim - high], axis=0).astype(bf16)

    def prepare():
        for j in range(3):
            arrive(lpart.at[j], l_recv.at[0, j])
            high, low = split2(lpart[j])
            ll[1 + j, 0:ROWS] = high
            ll[1 + j, ROWS : 2 * ROWS] = low

    def prepare_rims():
        ll[0, 2 * ROWS :] = both_parts(lmerged[:, part_of(x)])
        for j in range(3):
            arrive(lrimpart.at[j], l_recv.at[1, j])
            ll[1 + j, 2 * ROWS :] = both_parts(lrimpart[j])

    def prepare_column():
        arrive(crim.at[0], once_recv.at[7])
        arrive(crim.at[0], once_recv.at[8])
        cx[...] = both_parts(merge_y(crim[0], crim[1]))

    def spread_y(merged):
        return jnp.concatenate([merged, jnp.zeros((COLS - 16, COLS), f32), merged], axis=0).T

    def rim_y(left, right):
        return spread_y(merge_y(left, right))

    def residuals():
        arrive(rin.at[pl.ds(0, NGY - 1)], once_recv.at[9])
        lane8 = iota((8, COLS), 1)
        halves = []
        for half in range(2):
            record = rin[half * 8]
            for k in range(1, 8):
                record = jnp.where(lax.shift_right_logical(lane8, 4) == k, rin[half * 8 + k], record)
            halves.append(record)
        returned = jnp.concatenate(halves, axis=1)
        pieces = jnp.concatenate([p.astype(f32) for p in split3(returned)], axis=0).astype(bf16)
        found = dot(pieces, onehot[...])
        residual_out[...] = found[0:4] + found[8:12] + found[16:20]

    def left_step(s):
        arrive(ebuf.at[s, pl.ds(0, NZ_CHIPS - 1)], e_send.at[s])
        arrive(pout.at[s], p_send.at[s])
        arrive(qout.at[s], q_send.at[s])
        arrive(nbuf.at[s, pl.ds(0, NGY - 1)], n_send.at[s])
        arrive(eedge.at[s, pl.ds(0, NZ_CHIPS - 1)], ee_send.at[s])
        arrive(nedge.at[s, pl.ds(0, NGY - 1)], ne_send.at[s])
        arrive(xh_out.at[s], xh_send.at[s])
        arrive(yh_out.at[s], yh_send.at[s])

    def left_once():
        arrive(lpart, l_send.at[0])
        arrive(lrimpart, l_send.at[1])
        arrive(tx_in, once_send.at[0])
        arrive(ty_out, once_send.at[1])
        arrive(gout.at[pl.ds(0, NGY - 1)], once_send.at[2])
        arrive(lrim, once_send.at[3])
        arrive(crim, once_send.at[4])
        arrive(rout.at[pl.ds(0, NGY - 1)], once_send.at[5])

    def step(s, carry):
        t = STEPS - 1 - s
        def keep(at, block):
            high, low = split2(block)
            rows = pl.ds(pl.multiple_of(at * ROWS, ROWS), ROWS)
            ez[rows, 0:COLS] = high
            ez[rows, COLS : 2 * COLS] = low

        def from_z(i):
            at = wrap(z - RING[i], NZ_CHIPS)
            arrive(ebuf.at[s, at], e_recv.at[s, i])
            keep(at, ebuf[s, at])

        def from_y(i):
            block = nbuf.at[s, core * NY_CHIPS + wrap(y - RING[i], NY_CHIPS)]
            arrive(block, n_yrecv.at[s, i])
            send(block, block, n_send.at[s], n_crecv.at[s], sibling)

        keep(z, ebuf[s, z])
        arrive(yh_in.at[s, 0], yh_recv.at[s, 0])
        arrive(yh_in.at[s, 0], yh_recv.at[s, 1])
        eedge[s, z] = merge_y(yh_in[s, 0], yh_in[s, 1])
        for d in RING:
            send(eedge.at[s, z], eedge.at[s, z], ee_send.at[s], ee_recv.at[s], at_z(d))
        arrive(xh_in.at[s, 0], xh_recv.at[s, 0])
        arrive(xh_in.at[s, 1], xh_recv.at[s, 1])
        nedge[s, nslot] = merge_x(xh_in[s, 0, 1], xh_in[s, 1, 1])
        for d in RING:
            send(nedge.at[s, nslot], nedge.at[s, nslot], ne_send.at[s], ne_recv.at[s, 0], at_y(d))

        @pl.when(s == 0)
        def _():
            pass_rims()

        from_y(0)
        from_y(1)
        from_z(0)
        from_z(1)
        from_y(2)
        from_y(3)
        from_z(2)
        from_z(3)

        @pl.when(s == 0)
        def _():
            split_once()

        from_z(4)
        from_z(5)
        from_z(6)

        @pl.when(s == 0)
        def _():
            prepare()

        def side_share(slot):
            return turned_rim(dot_nt(ae[...], ll[slot, 0 : 2 * ROWS, :]))

        def line_share(slot):
            return dot(ll[slot, 0 : 2 * ROWS], ez[...])

        def rim_share(slot):
            return dot(ll[slot, 2 * ROWS :], ez[...])

        def inner_of(product):
            left, right = product[:, 0:COLS], product[:, COLS:]
            return left[0:ROWS] + (right[0:ROWS] + left[ROWS : 2 * ROWS])

        def rim_of(product, at):
            left, right = product[:, 0:COLS], product[:, COLS:]
            return left[at : at + 8] + (right[at : at + 8] + left[at + 8 : at + 16])

        def turned_rim(product):
            return product[0:8] + (pltpu.roll(product[0:8], ROWS, 1) + product[8:16])

        for j in (2, 0, 1):
            pout[s, j] = inner_of(line_share(1 + j))
            send(pout.at[s, j], pin.at[s, j], p_send.at[s], p_recv.at[s, j], at_x(-XS[j]))

        @pl.when(s == 0)
        def _():
            prepare_rims()

        arrive(eedge.at[s, pl.ds(0, NZ_CHIPS - 1)], ee_recv.at[s])
        lane = iota((8, COLS), 1)
        for k in range(NZ_CHIPS // 2):
            rim = jnp.where(lane < ROWS, pltpu.roll(eedge[s, 2 * k], ROWS, 1), eedge[s, 2 * k + 1])
            ae[:, k * COLS : (k + 1) * COLS] = both_parts(rim)
        for j in (2, 0, 1):
            qout[s, j, 0:8] = rim_of(rim_share(1 + j), 0)
            qout[s, j, 8:16] = side_share(1 + j)
            send(qout.at[s, j], qin.at[s, j], q_send.at[s], q_recv.at[s, j], at_x(-XS[j]))
        from_y(4)
        from_y(5)
        from_y(6)
        arrive(nedge.at[s, pl.ds(0, NY_CHIPS - 1)], ne_recv.at[s, 0])
        column_edges = nedge.at[s, pl.ds(core * NY_CHIPS, NY_CHIPS)]
        send(column_edges, column_edges, ne_send.at[s], ne_recv.at[s, 1], sibling)
        line_adjoint = inner_of(line_share(0))
        line_x = rim_of(rim_share(0), 0)
        line_y = side_share(0)

        @pl.when(s == 0)
        def _():
            arrive(tx_in.at[0], once_recv.at[0])
            arrive(tx_in.at[0], once_recv.at[1])
            arrive(ty_in.at[0], once_recv.at[2])
            arrive(ty_in.at[0], once_recv.at[3])
            prepare_column()
            gauges()

        surface = surf[...]
        east, north = traj[t, 1], traj[t, 2]
        whole = depth[...] + traj[t, 0]
        rim_surface = rim_y(yh_in[s, 0], yh_in[s, 1])[0:ROWS]
        flux_x = mass_rate * slope_x(surface, merge_x(xh_in[s, 0, 0], xh_in[s, 1, 0]))
        flux_y = mass_rate * slope_y(surface, rim_surface)
        gain = east * flux_x + north * flux_y
        depth_out[...] = jnp.where(s == 0, 0.0, depth_out[...]) + gain
        base[0] = surface + gain
        base[1] = whole * flux_x
        base[2] = whole * flux_y
        rims = rim_y(ty_in[0, t], ty_in[1, t])
        east_x = merge_x(tx_in[0, t, 0], tx_in[1, t, 0])
        north_x = merge_x(tx_in[0, t, 1], tx_in[1, t, 1])
        north_y = rims[ROWS:]
        coef[0] = 1.0 - advect_rate * slope_x(east, east_x)
        coef[1] = advect_rate * slope_x(north, north_x)
        coef[2] = advect_rate * slope_y(east, rims[0:ROWS])
        coef[3] = 1.0 - advect_rate * slope_y(north, north_y)

        arrive(nbuf.at[s, pl.ds(0, NY_CHIPS)], n_crecv.at[s])
        arrive(nedge.at[s, pl.ds(0, NY_CHIPS)], ne_recv.at[s, 1])
        for k in range(NGY):
            at = ((k % NY_CHIPS) * 2 + k // NY_CHIPS) * COLS
            at = slice(at, at + COLS)
            high, low = split2(nbuf[s, k])
            nn[0:ROWS, at] = high
            nn[ROWS : 2 * ROWS, at] = low
            nn[2 * ROWS : 2 * ROWS + 16, at] = both_parts(nedge[s, k])
        product = dot(nn[...], ct[...])
        column_adjoint, column_x = inner_of(product), rim_of(product, 2 * ROWS)
        column_y = spread_y(turned_rim(dot_nt(cx[...], nn[0 : 2 * ROWS, :])))[0:ROWS]

        @pl.when(s > 0)
        def _():
            left_step(s - 1)

        @pl.when(s == 2)
        def _():
            residuals()
            left_once()

        for j in range(3):
            arrive(qin.at[s, j], q_recv.at[s, j])
            line_x += qin[s, j, 0:8]
            line_y += qin[s, j, 8:16]
        line_y = spread_y(line_y)[0:ROWS]
        for j in range(3):
            arrive(pin.at[s, j], p_recv.at[s, j])
            line_adjoint += pin[s, j]

        along_x = slope_x(line_adjoint, line_x)
        along_y = slope_y(column_adjoint, column_y)
        mixed = slope_x(east * line_adjoint, east_x * line_x) + slope_y(
            north * line_adjoint, north_y * line_y
        )
        ebuf[s + 1, z] = (
            line_adjoint * coef[0] - column_adjoint * coef[1] + advect_rate * mixed + base[1]
        )

        surf[...] = base[0] + forcing[t] + slope_rate * (along_x + along_y)
        mixed = slope_x(east * column_adjoint, east_x * column_x) + slope_y(
            north * column_adjoint, north_y * column_y
        )
        nbuf[s + 1, nslot] = (
            column_adjoint * coef[3] - line_adjoint * coef[2] + advect_rate * mixed + base[2]
        )

        @pl.when(s < STEPS - 1)
        def _():
            send_x_rims(s + 1)
            send_z(s + 1, (6, 5, 4, 3, 2, 1, 0))
            send_rims(s + 1)
            send_y(s + 1)

        return carry

    for i in range(3):
        loads[i].wait()
    pl.semaphore_wait(barrier, len(peers))
    send_x_rims(0)
    loads[5].wait()
    send(line.at[pl.ds(0, 8)], lrim.at[1], once_send.at[3], once_recv.at[5], above)
    send(line.at[pl.ds(ROWS - 8, 8)], lrim.at[0], once_send.at[3], once_recv.at[6], below)
    send_z(0, (6, 5, 4, 3, 2, 1, 0))
    send_rims(0)
    send_y(0)
    start_once()
    lax.fori_loop(0, STEPS, step, 0)

    state_out[0] = surf[...]
    state_out[1] = ebuf[STEPS, z]
    state_out[2] = nbuf[STEPS, nslot]

    left_step(STEPS - 1)


def hand_over(state_in, depth_in, residual_in, state_out, depth_out, residual_out):
    state_out[...] = state_in[...]
    depth_out[...] = depth_in[...]
    residual_out[...] = residual_in[...]


def per_device(
    trajectory,
    depth,
    cotangent,
    line_inverse,
    column_inverse,
    gauge_owner,
    gauge_cell,
    gauge_obs,
    gauge_weight,
):
    vmem = pltpu.VMEM
    dma = pltpu.SemaphoreType.DMA
    scratch = [
        vmem((STEPS, 3, ROWS, COLS), f32),
        vmem((ROWS, COLS), f32),
        vmem((ROWS, 2048), f32),
        vmem((COLS, 2048), f32),
        vmem((1, COLS), jnp.int32),
        vmem((1, COLS), jnp.int32),
        vmem((STEPS, COLS), f32),
        vmem((1, COLS), f32),
        vmem((ROWS, COLS), f32),
        vmem((STEPS + 1, NZ_CHIPS, ROWS, COLS), f32),
        vmem((STEPS + 1, NGY, ROWS, COLS), f32),
        vmem((STEPS, NZ_CHIPS, 8, COLS), f32),
        vmem((STEPS, NGY, 8, COLS), f32),
        vmem((STEPS, 2, 2, 8, COLS), f32),
        vmem((STEPS, 2, 2, 8, COLS), f32),
        vmem((STEPS, 2, 8, COLS), f32),
        vmem((STEPS, 2, 8, COLS), f32),
        vmem((2, 8, 2048), f32),
        vmem((2, 8, 2048), f32),
        vmem((2, STEPS, 2, 8, COLS), f32),
        vmem((2, STEPS, 8, COLS), f32),
        vmem((2, STEPS, 8, COLS), f32),
        vmem((NGY, 8, COLS), f32),
        vmem((NGY, 8, COLS), f32),
        vmem((NGY, 8, COLS), f32),
        vmem((NGY, 8, COLS), f32),
        vmem((3, ROWS, 512), f32),
        vmem((3, 8, 512), f32),
        vmem((8, 2048), f32),
        vmem((STEPS, 3, ROWS, COLS), f32),
        vmem((STEPS, 3, ROWS, COLS), f32),
        vmem((STEPS, 3, 16, COLS), f32),
        vmem((STEPS, 3, 16, COLS), f32),
        vmem((2 * COLS, COLS), bf16),
        vmem((4, 2 * ROWS + 16, 512), bf16),
        vmem((2048, 2 * COLS), bf16),
        vmem((16, 2048), bf16),
        vmem((2 * ROWS + 16, 2048), bf16),
        vmem((16, 512), bf16),
        vmem((512, 2 * COLS), bf16),
        vmem((3 * STEPS * ROWS, COLS), bf16),
        vmem((STEPS, ROWS, COLS), f32),
        vmem((3, ROWS, COLS), f32),
        vmem((4, ROWS, COLS), f32),
        dma((11,)),
        dma((STEPS,)),
        dma((STEPS, 7)),
        dma((STEPS,)),
        dma((STEPS, 3)),
        dma((STEPS,)),
        dma((STEPS, 3)),
        dma((STEPS,)),
        dma((STEPS, 7)),
        dma((STEPS,)),
        dma((STEPS,)),
        dma((STEPS,)),
        dma((STEPS,)),
        dma((STEPS, 2)),
        dma((STEPS,)),
        dma((STEPS, 2)),
        dma((STEPS,)),
        dma((STEPS, 2)),
        dma((2,)),
        dma((2, 3)),
        dma((6,)),
        dma((10,)),
    ]
    anywhere = pl.BlockSpec(memory_space=pl.ANY)
    here = pl.BlockSpec(memory_space=pltpu.VMEM)
    results = pl.pallas_call(
        kernel,
        name="adjoint",
        out_shape=(
            jax.ShapeDtypeStruct((3, ROWS, COLS), f32),
            jax.ShapeDtypeStruct((ROWS, COLS), f32),
            jax.ShapeDtypeStruct((STEPS, COLS), f32),
        ),
        in_specs=[anywhere] * 9,
        out_specs=(here, here, here),
        scratch_shapes=scratch,
        compiler_params=pltpu.CompilerParams(
            collective_id=0, has_side_effects=True, vmem_limit_bytes=60 * 2**20
        ),
    )(
        trajectory,
        depth,
        cotangent,
        line_inverse,
        column_inverse,
        gauge_owner.reshape(1, COLS),
        gauge_cell.reshape(1, COLS),
        gauge_obs,
        gauge_weight.reshape(1, COLS),
    )
    return pl.pallas_call(
        hand_over,
        name="hand_over",
        out_shape=tuple(jax.ShapeDtypeStruct(r.shape, r.dtype) for r in results),
        in_specs=[here] * 3,
        out_specs=(here, here, here),
    )(*results)


def solution(mesh):
    return jax.shard_map(
        per_device,
        mesh=mesh,
        in_specs=(
            P(None, None, "gx", "gy"),
            P("gx", "gy"),
            P(None, "gx", "gy"),
            P("gx", None),
            P("gy", None),
            P(("gx", "gy"), None),
            P(("gx", "gy")),
            P(None, ("gx", "gy")),
            P(("gx", "gy")),
        ),
        out_specs=(P(None, "gx", "gy"), P("gx", "gy"), P(None, ("gx", "gy"))),
        check_vma=False,
    )
```

```python
import functools

import jax
import jax.numpy as jnp
from jax import lax
from jax.experimental import pallas as pl
from jax.experimental.pallas import tpu as pltpu
from jax.sharding import PartitionSpec as P

mass_rate = 0.25
slope_rate = 0.3
advect_rate = 0.2
MESH = pl.DeviceIdType.MESH
f32 = jnp.float32
bf16 = jnp.bfloat16

NX_CHIPS, NZ_CHIPS, NY_CHIPS = 4, 8, 8
NGX, NGY = 32, 16
STEPS, ROWS, COLS = 4, 64, 128
XS = (1, -1, 2)
RING = (1, -1, 2, -2, 3, -3, 4)


def wrap(value, count):
    return lax.rem(value + count, count)


def split2(value):
    high = value.astype(bf16)
    low = (value - high.astype(f32)).astype(bf16)
    return high, low


def split3(value):
    first = value.astype(bf16)
    rest = value - first.astype(f32)
    second = rest.astype(bf16)
    third = (rest - second.astype(f32)).astype(bf16)
    return first, second, third


def dot(a, b):
    return lax.dot_general(a, b, (((1,), (0,)), ((), ())), preferred_element_type=f32)


def dot_nt(a, b):
    return lax.dot_general(a, b, (((1,), (1,)), ((), ())), preferred_element_type=f32)


def iota(shape, dim):
    return lax.broadcasted_iota(jnp.int32, shape, dim)


def slope_x(field, rim):
    padded = jnp.concatenate([rim, field, rim], axis=0)
    count = padded.shape[0]

    def window(shift):
        return pltpu.roll(padded, shift, 0)[8 : 8 + ROWS]

    return (window(2) - window(count - 2) + 8.0 * (window(count - 1) - window(1))) * (1.0 / 12.0)


def slope_y(field, rim):
    lane = iota(field.shape, 1)
    outer = pltpu.roll(jnp.where(lane >= COLS - 2, rim, field), 2, 1) - pltpu.roll(
        jnp.where(lane < 2, rim, field), COLS - 2, 1
    )
    inner = pltpu.roll(jnp.where(lane < 1, rim, field), COLS - 1, 1) - pltpu.roll(
        jnp.where(lane >= COLS - 1, rim, field), 1, 1
    )
    return (outer + 8.0 * inner) * (1.0 / 12.0)


def kernel(
    traj_in,
    depth_in,
    cot_in,
    line_in,
    column_in,
    owner_in,
    cell_in,
    obs_in,
    weight_in,
    state_out,
    depth_out,
    residual_out,
    traj,
    depth,
    line,
    column,
    owner,
    cell,
    obs,
    weight,
    surf,
    ebuf,
    nbuf,
    eedge,
    nedge,
    xh_out,
    xh_in,
    yh_out,
    yh_in,
    lrim,
    crim,
    tx_in,
    ty_out,
    ty_in,
    gout,
    gin,
    rout,
    rin,
    lpart,
    lrimpart,
    lmerged,
    pout,
    pin,
    qout,
    qin,
    onehot,
    ll,
    ct,
    cx,
    nn,
    ae,
    ez,
    fields3,
    forcing,
    base,
    coef,
    load_sem,
    e_send,
    e_recv,
    p_send,
    p_recv,
    q_send,
    q_recv,
    n_send,
    n_yrecv,
    n_crecv,
    ee_send,
    ee_recv,
    ne_send,
    ne_recv,
    xh_send,
    xh_recv,
    yh_send,
    yh_recv,
    l_send,
    l_recv,
    once_send,
    once_recv,
):
    gx = lax.axis_index("gx")
    gy = lax.axis_index("gy")
    x, z = lax.div(gx, NZ_CHIPS), lax.rem(gx, NZ_CHIPS)
    y, core = lax.div(gy, 2), lax.rem(gy, 2)
    nslot = core * NY_CHIPS + y

    def at_x(d):
        return (wrap(x + d, NX_CHIPS) * NZ_CHIPS + z, gy)

    def at_z(d):
        return (x * NZ_CHIPS + wrap(z + d, NZ_CHIPS), gy)

    def at_y(d):
        return (gx, wrap(y + d, NY_CHIPS) * 2 + core)

    sibling = (gx, y * 2 + 1 - core)
    above, below = (wrap(gx - 1, NGX), gy), (wrap(gx + 1, NGX), gy)
    before, after = (gx, wrap(gy - 1, NGY)), (gx, wrap(gy + 1, NGY))

    has_above = jnp.where(gx > 0, 1.0, 0.0).astype(f32)
    has_below = jnp.where(gx < NGX - 1, 1.0, 0.0).astype(f32)
    has_before = jnp.where(gy > 0, 1.0, 0.0).astype(f32)
    has_after = jnp.where(gy < NGY - 1, 1.0, 0.0).astype(f32)

    def merge_x(top, bottom):
        return jnp.where(iota(top.shape, 0) >= 4, top * has_above, bottom * has_below)

    def merge_y(left, right):
        return jnp.where(iota(left.shape, 0) >= 4, left * has_before, right * has_after)

    def send(src, dst, send_sem, recv_sem, device):
        pltpu.make_async_remote_copy(
            src_ref=src,
            dst_ref=dst,
            send_sem=send_sem,
            recv_sem=recv_sem,
            device_id=device,
            device_id_type=MESH,
        ).start()

    def arrive(ref, sem):
        pltpu.make_async_copy(ref, ref, sem).wait()

    loads = [
        pltpu.make_async_copy(src, dst, load_sem.at[i])
        for i, (src, dst) in enumerate(
            [
                (cot_in.at[0], surf),
                (cot_in.at[1], ebuf.at[0, z]),
                (cot_in.at[2], nbuf.at[0, nslot]),
                (traj_in, traj),
                (depth_in, depth),
                (line_in, line),
                (column_in, column),
                (owner_in, owner),
                (cell_in, cell),
                (obs_in, obs),
                (weight_in, weight),
            ]
        )
    ]

    barrier = pltpu.get_barrier_semaphore()
    peers = (
        [at_z(d) for d in reversed(RING)]
        + [(gx, lax.rem(gy + d, NGY)) for d in (8, 9, 7, 10, 6, 11, 5, 12, 4, 13, 3, 14, 2, 15, 1)]
        + [at_x(d) for d in reversed(XS)]
        + [above, below]
    )
    for peer in peers:
        pl.semaphore_signal(barrier, inc=1, device_id=peer, device_id_type=MESH)
    for copy in loads:
        copy.start()
    part = NZ_CHIPS * ROWS

    def part_of(at):
        return pl.ds(pl.multiple_of(at * part, part), part)

    def pack_gauges():
        owners = owner[...]
        member = jnp.where(iota((NGY, COLS), 0) == owners, 1.0, 0.0).astype(f32)
        upper = jnp.where(iota((COLS, COLS), 0) <= iota((COLS, COLS), 1), 1.0, 0.0).astype(bf16)
        counted = dot(member.astype(bf16), upper)
        rank = jnp.sum(counted * member, axis=0, keepdims=True).astype(jnp.int32) - 1
        target = owners * 16 + rank
        picked = jnp.where(iota((2 * COLS, COLS), 0) == target, 1.0, 0.0).astype(bf16)
        onehot[...] = picked
        cells = cell[...]
        row = lax.shift_right_logical(cells, 7).astype(f32)
        col = lax.bitwise_and(cells, COLS - 1).astype(f32)
        payload = jnp.concatenate([obs[...], weight[...], row, col, jnp.ones_like(row)], axis=0)
        parts = jnp.concatenate([p.astype(f32) for p in split3(payload)], axis=0).astype(bf16)
        placed = dot_nt(parts, picked)
        placed = placed[0:8] + placed[8:16] + placed[16:24]
        mod = lax.rem(gy, 8)
        for d in range(NGY):
            half = placed[:, (d // 8) * COLS : (d // 8 + 1) * COLS]
            gout[d] = pltpu.roll(half, wrap(mod - d % 8, 8) * 16, 1)

    def split_once():
        high, low = split2(line[:, part_of(x)])
        ll[0, 0:ROWS] = high
        ll[0, ROWS : 2 * ROWS] = low
        for k in range(NGY):
            at = slice(k * COLS, (k + 1) * COLS)
            high, low = split2(column[:, at].T)
            ct[at, 0:COLS] = high
            ct[at, COLS : 2 * COLS] = low
        for t in range(STEPS):
            for p, piece in enumerate(split3(traj[t, 0])):
                fields3[pl.ds((p * STEPS + t) * ROWS, ROWS)] = piece

    def send_z(s, these):
        mine = ebuf.at[s, z]
        for i in these:
            send(mine, mine, e_send.at[s], e_recv.at[s, i], at_z(RING[i]))

    def send_rims(s):
        surface = surf[...]
        turned = jnp.concatenate([surface, ebuf[s, z]], axis=0).T
        yh_out[s, 0] = turned[0:8]
        yh_out[s, 1] = turned[COLS - 8 :]
        send(yh_out.at[s, 0], yh_in.at[s, 1], yh_send.at[s], yh_recv.at[s, 1], before)
        send(yh_out.at[s, 1], yh_in.at[s, 0], yh_send.at[s], yh_recv.at[s, 0], after)

    def send_x_rims(s):
        surface = surf[...]
        north = nbuf[s, nslot]
        xh_out[s, 0, 0] = surface[0:8]
        xh_out[s, 0, 1] = north[0:8]
        xh_out[s, 1, 0] = surface[ROWS - 8 :]
        xh_out[s, 1, 1] = north[ROWS - 8 :]
        send(xh_out.at[s, 0], xh_in.at[s, 1], xh_send.at[s], xh_recv.at[s, 1], above)
        send(xh_out.at[s, 1], xh_in.at[s, 0], xh_send.at[s], xh_recv.at[s, 0], below)

    def send_y(s):
        own = nbuf.at[s, nslot]
        for i in (6, 5, 4, 3, 2, 1, 0):
            send(own, own, n_send.at[s], n_yrecv.at[s, i], at_y(RING[i]))
        send(own, own, n_send.at[s], n_crecv.at[s], sibling)

    def start_once():
        for j, d in enumerate(XS):
            piece = line.at[:, part_of(wrap(x + d, NX_CHIPS))]
            send(piece, lpart.at[j], l_send.at[0], l_recv.at[0, j], at_x(d))
        for i in (3, 4, 6, 7, 8, 9, 10):
            loads[i].wait()
        send(column.at[pl.ds(0, 8)], crim.at[1], once_send.at[4], once_recv.at[7], before)
        send(column.at[pl.ds(COLS - 8, 8)], crim.at[0], once_send.at[4], once_recv.at[8], after)
        pack_gauges()
        gin[gy] = gout[gy]
        for d in range(1, NGY):
            peer = lax.rem(gy + d, NGY)
            send(gout.at[peer], gin.at[gy], once_send.at[2], once_recv.at[4], (gx, peer))
        both = pl.ds(1, 2)
        send(traj.at[:, both, pl.ds(0, 8)], tx_in.at[1], once_send.at[0], once_recv.at[0], above)
        send(
            traj.at[:, both, pl.ds(ROWS - 8, 8)],
            tx_in.at[0],
            once_send.at[0],
            once_recv.at[1],
            below,
        )
        for t in range(STEPS):
            turned = jnp.concatenate([traj[t, 1], traj[t, 2]], axis=0).T
            ty_out[0, t] = turned[0:8]
            ty_out[1, t] = turned[COLS - 8 :]
        send(ty_out.at[0], ty_in.at[1], once_send.at[1], once_recv.at[2], before)
        send(ty_out.at[1], ty_in.at[0], once_send.at[1], once_recv.at[3], after)

    def gauges():
        arrive(gin.at[pl.ds(0, NGY - 1)], once_recv.at[4])
        mod = lax.rem(gy, 8)
        lane8 = iota((8, COLS), 1)
        total = None
        for half in range(2):
            record = gin[half * 8]
            for k in range(1, 8):
                record = jnp.where(lax.shift_right_logical(lane8, 4) == k, gin[half * 8 + k], record)
            valid = record[7:8] > 0.5
            row = record[5:6].astype(jnp.int32)
            col = record[6:7].astype(jnp.int32)
            in_col = jnp.where((iota((COLS, COLS), 0) == col) & valid, 1.0, 0.0).astype(bf16)
            in_row = jnp.where(iota((ROWS, COLS), 0) == row, 1.0, 0.0).astype(f32)
            seen = dot(fields3[...], in_col)
            misfits, parts = [], [[], [], []]
            for t in range(STEPS):
                at = [seen[(p * STEPS + t) * ROWS : (p * STEPS + t + 1) * ROWS] for p in range(3)]
                value = jnp.sum((at[0] + at[1] + at[2]) * in_row, axis=0, keepdims=True)
                misfit = jnp.where(valid, value - record[t : t + 1], 0.0)
                misfits.append(misfit)
                for p, piece in enumerate(split3(record[4:5] * misfit)):
                    parts[p].append((in_row * piece.astype(f32)).astype(bf16))
            back = jnp.concatenate(misfits + [jnp.zeros((4, COLS), f32)], axis=0)
            for k in range(8):
                rout[half * 8 + k] = pltpu.roll(back, wrap(mod - k, 8) * 16, 1)
            spread = dot_nt(jnp.concatenate(parts[0] + parts[1] + parts[2], axis=0), in_col)
            total = spread if total is None else total + spread
        size = STEPS * ROWS
        total = total[0:size] + total[size : 2 * size] + total[2 * size :]
        for t in range(STEPS):
            forcing[t] = total[t * ROWS : (t + 1) * ROWS]
        rin[gy] = rout[gy]
        for d in range(1, NGY):
            peer = lax.rem(gy + d, NGY)
            send(rout.at[peer], rin.at[gy], once_send.at[5], once_recv.at[9], (gx, peer))

    def pass_rims():
        arrive(lrim.at[0], once_recv.at[5])
        arrive(lrim.at[0], once_recv.at[6])
        lmerged[...] = merge_x(lrim[0], lrim[1])
        for j, d in enumerate(XS):
            piece = lmerged.at[:, part_of(wrap(x + d, NX_CHIPS))]
            send(piece, lrimpart.at[j], l_send.at[1], l_recv.at[1, j], at_x(d))

    def both_parts(rim):
        high = rim.astype(bf16).astype(f32)
        return jnp.concatenate([high, rim - high], axis=0).astype(bf16)

    def prepare():
        for j in range(3):
            arrive(lpart.at[j], l_recv.at[0, j])
            high, low = split2(lpart[j])
            ll[1 + j, 0:ROWS] = high
            ll[1 + j, ROWS : 2 * ROWS] = low

    def prepare_rims():
        ll[0, 2 * ROWS :] = both_parts(lmerged[:, part_of(x)])
        for j in range(3):
            arrive(lrimpart.at[j], l_recv.at[1, j])
            ll[1 + j, 2 * ROWS :] = both_parts(lrimpart[j])

    def prepare_column():
        arrive(crim.at[0], once_recv.at[7])
        arrive(crim.at[0], once_recv.at[8])
        cx[...] = both_parts(merge_y(crim[0], crim[1]))

    def spread_y(merged):
        return jnp.concatenate([merged, jnp.zeros((COLS - 16, COLS), f32), merged], axis=0).T

    def rim_y(left, right):
        return spread_y(merge_y(left, right))

    def residuals():
        arrive(rin.at[pl.ds(0, NGY - 1)], once_recv.at[9])
        lane8 = iota((8, COLS), 1)
        halves = []
        for half in range(2):
            record = rin[half * 8]
            for k in range(1, 8):
                record = jnp.where(lax.shift_right_logical(lane8, 4) == k, rin[half * 8 + k], record)
            halves.append(record)
        returned = jnp.concatenate(halves, axis=1)
        pieces = jnp.concatenate([p.astype(f32) for p in split3(returned)], axis=0).astype(bf16)
        found = dot(pieces, onehot[...])
        residual_out[...] = found[0:4] + found[8:12] + found[16:20]

    def left_step(s):
        arrive(ebuf.at[s, pl.ds(0, NZ_CHIPS - 1)], e_send.at[s])
        arrive(pout.at[s], p_send.at[s])
        arrive(qout.at[s], q_send.at[s])
        arrive(nbuf.at[s, pl.ds(0, NGY - 1)], n_send.at[s])
        arrive(eedge.at[s, pl.ds(0, NZ_CHIPS - 1)], ee_send.at[s])
        arrive(nedge.at[s, pl.ds(0, NGY - 1)], ne_send.at[s])
        arrive(xh_out.at[s], xh_send.at[s])
        arrive(yh_out.at[s], yh_send.at[s])

    def left_once():
        arrive(lpart, l_send.at[0])
        arrive(lrimpart, l_send.at[1])
        arrive(tx_in, once_send.at[0])
        arrive(ty_out, once_send.at[1])
        arrive(gout.at[pl.ds(0, NGY - 1)], once_send.at[2])
        arrive(lrim, once_send.at[3])
        arrive(crim, once_send.at[4])
        arrive(rout.at[pl.ds(0, NGY - 1)], once_send.at[5])

    def step(s, carry):
        t = STEPS - 1 - s
        def keep(at, block):
            high, low = split2(block)
            rows = pl.ds(pl.multiple_of(at * ROWS, ROWS), ROWS)
            ez[rows, 0:COLS] = high
            ez[rows, COLS : 2 * COLS] = low

        def from_z(i):
            at = wrap(z - RING[i], NZ_CHIPS)
            arrive(ebuf.at[s, at], e_recv.at[s, i])
            keep(at, ebuf[s, at])

        def from_y(i):
            block = nbuf.at[s, core * NY_CHIPS + wrap(y - RING[i], NY_CHIPS)]
            arrive(block, n_yrecv.at[s, i])
            send(block, block, n_send.at[s], n_crecv.at[s], sibling)

        keep(z, ebuf[s, z])
        arrive(yh_in.at[s, 0], yh_recv.at[s, 0])
        arrive(yh_in.at[s, 0], yh_recv.at[s, 1])
        eedge[s, z] = merge_y(yh_in[s, 0], yh_in[s, 1])
        for d in RING:
            send(eedge.at[s, z], eedge.at[s, z], ee_send.at[s], ee_recv.at[s], at_z(d))
        arrive(xh_in.at[s, 0], xh_recv.at[s, 0])
        arrive(xh_in.at[s, 1], xh_recv.at[s, 1])
        nedge[s, nslot] = merge_x(xh_in[s, 0, 1], xh_in[s, 1, 1])
        for d in RING:
            send(nedge.at[s, nslot], nedge.at[s, nslot], ne_send.at[s], ne_recv.at[s, 0], at_y(d))

        @pl.when(s == 0)
        def _():
            pass_rims()

        from_y(0)
        from_y(1)
        from_z(0)
        from_z(1)
        from_y(2)
        from_y(3)
        from_z(2)
        from_z(3)

        @pl.when(s == 0)
        def _():
            split_once()

        from_z(4)
        from_z(5)
        from_z(6)

        @pl.when(s == 0)
        def _():
            prepare()

        def side_share(slot):
            return turned_rim(dot_nt(ae[...], ll[slot, 0 : 2 * ROWS, :]))

        def line_share(slot):
            return dot(ll[slot, 0 : 2 * ROWS], ez[...])

        def rim_share(slot):
            return dot(ll[slot, 2 * ROWS :], ez[...])

        def inner_of(product):
            left, right = product[:, 0:COLS], product[:, COLS:]
            return left[0:ROWS] + (right[0:ROWS] + left[ROWS : 2 * ROWS])

        def rim_of(product, at):
            left, right = product[:, 0:COLS], product[:, COLS:]
            return left[at : at + 8] + (right[at : at + 8] + left[at + 8 : at + 16])

        def turned_rim(product):
            return product[0:8] + (pltpu.roll(product[0:8], ROWS, 1) + product[8:16])

        for j in (2, 0, 1):
            pout[s, j] = inner_of(line_share(1 + j))
            send(pout.at[s, j], pin.at[s, j], p_send.at[s], p_recv.at[s, j], at_x(-XS[j]))

        @pl.when(s == 0)
        def _():
            prepare_rims()

        for j in (2, 0, 1):
            qout[s, j, 0:8] = rim_of(rim_share(1 + j), 0)
        line_adjoint = inner_of(line_share(0))
        line_x = rim_of(rim_share(0), 0)
        arrive(eedge.at[s, pl.ds(0, NZ_CHIPS - 1)], ee_recv.at[s])
        lane = iota((8, COLS), 1)
        for k in range(NZ_CHIPS // 2):
            rim = jnp.where(lane < ROWS, pltpu.roll(eedge[s, 2 * k], ROWS, 1), eedge[s, 2 * k + 1])
            ae[:, k * COLS : (k + 1) * COLS] = both_parts(rim)
        for j in (2, 0, 1):
            qout[s, j, 8:16] = side_share(1 + j)
            send(qout.at[s, j], qin.at[s, j], q_send.at[s], q_recv.at[s, j], at_x(-XS[j]))
        from_y(4)
        from_y(5)
        from_y(6)
        arrive(nedge.at[s, pl.ds(0, NY_CHIPS - 1)], ne_recv.at[s, 0])
        column_edges = nedge.at[s, pl.ds(core * NY_CHIPS, NY_CHIPS)]
        send(column_edges, column_edges, ne_send.at[s], ne_recv.at[s, 1], sibling)
        line_y = side_share(0)

        @pl.when(s == 0)
        def _():
            arrive(tx_in.at[0], once_recv.at[0])
            arrive(tx_in.at[0], once_recv.at[1])
            arrive(ty_in.at[0], once_recv.at[2])
            arrive(ty_in.at[0], once_recv.at[3])
            prepare_column()
            gauges()

        surface = surf[...]
        east, north = traj[t, 1], traj[t, 2]
        whole = depth[...] + traj[t, 0]
        rim_surface = rim_y(yh_in[s, 0], yh_in[s, 1])[0:ROWS]
        flux_x = mass_rate * slope_x(surface, merge_x(xh_in[s, 0, 0], xh_in[s, 1, 0]))
        flux_y = mass_rate * slope_y(surface, rim_surface)
        gain = east * flux_x + north * flux_y
        depth_out[...] = jnp.where(s == 0, 0.0, depth_out[...]) + gain
        base[0] = surface + gain
        base[1] = whole * flux_x
        base[2] = whole * flux_y
        rims = rim_y(ty_in[0, t], ty_in[1, t])
        east_x = merge_x(tx_in[0, t, 0], tx_in[1, t, 0])
        north_x = merge_x(tx_in[0, t, 1], tx_in[1, t, 1])
        north_y = rims[ROWS:]
        coef[0] = 1.0 - advect_rate * slope_x(east, east_x)
        coef[1] = advect_rate * slope_x(north, north_x)
        coef[2] = advect_rate * slope_y(east, rims[0:ROWS])
        coef[3] = 1.0 - advect_rate * slope_y(north, north_y)

        arrive(nbuf.at[s, pl.ds(0, NY_CHIPS)], n_crecv.at[s])
        arrive(nedge.at[s, pl.ds(0, NY_CHIPS)], ne_recv.at[s, 1])
        for k in range(NGY):
            at = ((k % NY_CHIPS) * 2 + k // NY_CHIPS) * COLS
            at = slice(at, at + COLS)
            high, low = split2(nbuf[s, k])
            nn[0:ROWS, at] = high
            nn[ROWS : 2 * ROWS, at] = low
            nn[2 * ROWS : 2 * ROWS + 16, at] = both_parts(nedge[s, k])
        product = dot(nn[...], ct[...])
        column_adjoint, column_x = inner_of(product), rim_of(product, 2 * ROWS)
        column_y = spread_y(turned_rim(dot_nt(cx[...], nn[0 : 2 * ROWS, :])))[0:ROWS]

        @pl.when(s > 0)
        def _():
            left_step(s - 1)

        @pl.when(s == 2)
        def _():
            residuals()
            left_once()

        for j in range(3):
            arrive(qin.at[s, j], q_recv.at[s, j])
            line_x += qin[s, j, 0:8]
            line_y += qin[s, j, 8:16]
        line_y = spread_y(line_y)[0:ROWS]
        for j in range(3):
            arrive(pin.at[s, j], p_recv.at[s, j])
            line_adjoint += pin[s, j]

        along_x = slope_x(line_adjoint, line_x)
        along_y = slope_y(column_adjoint, column_y)
        mixed = slope_x(east * line_adjoint, east_x * line_x) + slope_y(
            north * line_adjoint, north_y * line_y
        )
        ebuf[s + 1, z] = (
            line_adjoint * coef[0] - column_adjoint * coef[1] + advect_rate * mixed + base[1]
        )

        surf[...] = base[0] + forcing[t] + slope_rate * (along_x + along_y)
        mixed = slope_x(east * column_adjoint, east_x * column_x) + slope_y(
            north * column_adjoint, north_y * column_y
        )
        nbuf[s + 1, nslot] = (
            column_adjoint * coef[3] - line_adjoint * coef[2] + advect_rate * mixed + base[2]
        )

        @pl.when(s < STEPS - 1)
        def _():
            send_x_rims(s + 1)
            send_z(s + 1, (6, 5, 4, 3, 2, 1, 0))
            send_rims(s + 1)
            send_y(s + 1)

        return carry

    for i in range(3):
        loads[i].wait()
    pl.semaphore_wait(barrier, len(peers))
    send_x_rims(0)
    loads[5].wait()
    send(line.at[pl.ds(0, 8)], lrim.at[1], once_send.at[3], once_recv.at[5], above)
    send(line.at[pl.ds(ROWS - 8, 8)], lrim.at[0], once_send.at[3], once_recv.at[6], below)
    send_z(0, (6, 5, 4, 3, 2, 1, 0))
    send_rims(0)
    send_y(0)
    start_once()
    lax.fori_loop(0, STEPS, step, 0)

    state_out[0] = surf[...]
    state_out[1] = ebuf[STEPS, z]
    state_out[2] = nbuf[STEPS, nslot]

    left_step(STEPS - 1)


def hand_over(state_in, depth_in, residual_in, state_out, depth_out, residual_out):
    state_out[...] = state_in[...]
    depth_out[...] = depth_in[...]
    residual_out[...] = residual_in[...]


def per_device(
    trajectory,
    depth,
    cotangent,
    line_inverse,
    column_inverse,
    gauge_owner,
    gauge_cell,
    gauge_obs,
    gauge_weight,
):
    vmem = pltpu.VMEM
    dma = pltpu.SemaphoreType.DMA
    scratch = [
        vmem((STEPS, 3, ROWS, COLS), f32),
        vmem((ROWS, COLS), f32),
        vmem((ROWS, 2048), f32),
        vmem((COLS, 2048), f32),
        vmem((1, COLS), jnp.int32),
        vmem((1, COLS), jnp.int32),
        vmem((STEPS, COLS), f32),
        vmem((1, COLS), f32),
        vmem((ROWS, COLS), f32),
        vmem((STEPS + 1, NZ_CHIPS, ROWS, COLS), f32),
        vmem((STEPS + 1, NGY, ROWS, COLS), f32),
        vmem((STEPS, NZ_CHIPS, 8, COLS), f32),
        vmem((STEPS, NGY, 8, COLS), f32),
        vmem((STEPS, 2, 2, 8, COLS), f32),
        vmem((STEPS, 2, 2, 8, COLS), f32),
        vmem((STEPS, 2, 8, COLS), f32),
        vmem((STEPS, 2, 8, COLS), f32),
        vmem((2, 8, 2048), f32),
        vmem((2, 8, 2048), f32),
        vmem((2, STEPS, 2, 8, COLS), f32),
        vmem((2, STEPS, 8, COLS), f32),
        vmem((2, STEPS, 8, COLS), f32),
        vmem((NGY, 8, COLS), f32),
        vmem((NGY, 8, COLS), f32),
        vmem((NGY, 8, COLS), f32),
        vmem((NGY, 8, COLS), f32),
        vmem((3, ROWS, 512), f32),
        vmem((3, 8, 512), f32),
        vmem((8, 2048), f32),
        vmem((STEPS, 3, ROWS, COLS), f32),
        vmem((STEPS, 3, ROWS, COLS), f32),
        vmem((STEPS, 3, 16, COLS), f32),
        vmem((STEPS, 3, 16, COLS), f32),
        vmem((2 * COLS, COLS), bf16),
        vmem((4, 2 * ROWS + 16, 512), bf16),
        vmem((2048, 2 * COLS), bf16),
        vmem((16, 2048), bf16),
        vmem((2 * ROWS + 16, 2048), bf16),
        vmem((16, 512), bf16),
        vmem((512, 2 * COLS), bf16),
        vmem((3 * STEPS * ROWS, COLS), bf16),
        vmem((STEPS, ROWS, COLS), f32),
        vmem((3, ROWS, COLS), f32),
        vmem((4, ROWS, COLS), f32),
        dma((11,)),
        dma((STEPS,)),
        dma((STEPS, 7)),
        dma((STEPS,)),
        dma((STEPS, 3)),
        dma((STEPS,)),
        dma((STEPS, 3)),
        dma((STEPS,)),
        dma((STEPS, 7)),
        dma((STEPS,)),
        dma((STEPS,)),
        dma((STEPS,)),
        dma((STEPS,)),
        dma((STEPS, 2)),
        dma((STEPS,)),
        dma((STEPS, 2)),
        dma((STEPS,)),
        dma((STEPS, 2)),
        dma((2,)),
        dma((2, 3)),
        dma((6,)),
        dma((10,)),
    ]
    anywhere = pl.BlockSpec(memory_space=pl.ANY)
    here = pl.BlockSpec(memory_space=pltpu.VMEM)
    results = pl.pallas_call(
        kernel,
        name="adjoint",
        out_shape=(
            jax.ShapeDtypeStruct((3, ROWS, COLS), f32),
            jax.ShapeDtypeStruct((ROWS, COLS), f32),
            jax.ShapeDtypeStruct((STEPS, COLS), f32),
        ),
        in_specs=[anywhere] * 9,
        out_specs=(here, here, here),
        scratch_shapes=scratch,
        compiler_params=pltpu.CompilerParams(
            collective_id=0, has_side_effects=True, vmem_limit_bytes=60 * 2**20
        ),
    )(
        trajectory,
        depth,
        cotangent,
        line_inverse,
        column_inverse,
        gauge_owner.reshape(1, COLS),
        gauge_cell.reshape(1, COLS),
        gauge_obs,
        gauge_weight.reshape(1, COLS),
    )
    return pl.pallas_call(
        hand_over,
        name="hand_over",
        out_shape=tuple(jax.ShapeDtypeStruct(r.shape, r.dtype) for r in results),
        in_specs=[here] * 3,
        out_specs=(here, here, here),
    )(*results)


def solution(mesh):
    return jax.shard_map(
        per_device,
        mesh=mesh,
        in_specs=(
            P(None, None, "gx", "gy"),
            P("gx", "gy"),
            P(None, "gx", "gy"),
            P("gx", None),
            P("gy", None),
            P(("gx", "gy"), None),
            P(("gx", "gy")),
            P(None, ("gx", "gy")),
            P(("gx", "gy")),
        ),
        out_specs=(P(None, "gx", "gy"), P("gx", "gy"), P(None, ("gx", "gy"))),
        check_vma=False,
    )
```

```python
import functools

import jax
import jax.numpy as jnp
from jax import lax
from jax.experimental import pallas as pl
from jax.experimental.pallas import tpu as pltpu
from jax.sharding import PartitionSpec as P

mass_rate = 0.25
slope_rate = 0.3
advect_rate = 0.2
MESH = pl.DeviceIdType.MESH
f32 = jnp.float32
bf16 = jnp.bfloat16

NX_CHIPS, NZ_CHIPS, NY_CHIPS = 4, 8, 8
NGX, NGY = 32, 16
STEPS, ROWS, COLS = 4, 64, 128
XS = (1, -1, 2)
RING = (1, -1, 2, -2, 3, -3, 4)


def wrap(value, count):
    return lax.rem(value + count, count)


def split2(value):
    high = value.astype(bf16)
    low = (value - high.astype(f32)).astype(bf16)
    return high, low


def split3(value):
    first = value.astype(bf16)
    rest = value - first.astype(f32)
    second = rest.astype(bf16)
    third = (rest - second.astype(f32)).astype(bf16)
    return first, second, third


def dot(a, b):
    return lax.dot_general(a, b, (((1,), (0,)), ((), ())), preferred_element_type=f32)


def dot_nt(a, b):
    return lax.dot_general(a, b, (((1,), (1,)), ((), ())), preferred_element_type=f32)


def iota(shape, dim):
    return lax.broadcasted_iota(jnp.int32, shape, dim)


def slope_x(field, rim):
    padded = jnp.concatenate([rim, field, rim], axis=0)
    count = padded.shape[0]

    def window(shift):
        return pltpu.roll(padded, shift, 0)[8 : 8 + ROWS]

    return (window(2) - window(count - 2) + 8.0 * (window(count - 1) - window(1))) * (1.0 / 12.0)


def slope_y(field, rim):
    lane = iota(field.shape, 1)
    outer = pltpu.roll(jnp.where(lane >= COLS - 2, rim, field), 2, 1) - pltpu.roll(
        jnp.where(lane < 2, rim, field), COLS - 2, 1
    )
    inner = pltpu.roll(jnp.where(lane < 1, rim, field), COLS - 1, 1) - pltpu.roll(
        jnp.where(lane >= COLS - 1, rim, field), 1, 1
    )
    return (outer + 8.0 * inner) * (1.0 / 12.0)


def kernel(
    traj_in,
    depth_in,
    cot_in,
    line_in,
    column_in,
    owner_in,
    cell_in,
    obs_in,
    weight_in,
    state_out,
    depth_out,
    residual_out,
    traj,
    depth,
    line,
    column,
    owner,
    cell,
    obs,
    weight,
    surf,
    ebuf,
    nbuf,
    eedge,
    nedge,
    xh_out,
    xh_in,
    yh_out,
    yh_in,
    lrim,
    crim,
    tx_in,
    ty_out,
    ty_in,
    gout,
    gin,
    rout,
    rin,
    lpart,
    lrimpart,
    lmerged,
    pout,
    pin,
    qout,
    qin,
    onehot,
    ll,
    ct,
    cx,
    nn,
    ae,
    ez,
    fields3,
    forcing,
    base,
    coef,
    load_sem,
    e_send,
    e_recv,
    p_send,
    p_recv,
    q_send,
    q_recv,
    n_send,
    n_yrecv,
    n_crecv,
    ee_send,
    ee_recv,
    ne_send,
    ne_recv,
    xh_send,
    xh_recv,
    yh_send,
    yh_recv,
    l_send,
    l_recv,
    once_send,
    once_recv,
):
    gx = lax.axis_index("gx")
    gy = lax.axis_index("gy")
    x, z = lax.div(gx, NZ_CHIPS), lax.rem(gx, NZ_CHIPS)
    y, core = lax.div(gy, 2), lax.rem(gy, 2)
    nslot = core * NY_CHIPS + y

    def at_x(d):
        return (wrap(x + d, NX_CHIPS) * NZ_CHIPS + z, gy)

    def at_z(d):
        return (x * NZ_CHIPS + wrap(z + d, NZ_CHIPS), gy)

    def at_y(d):
        return (gx, wrap(y + d, NY_CHIPS) * 2 + core)

    sibling = (gx, y * 2 + 1 - core)
    above, below = (wrap(gx - 1, NGX), gy), (wrap(gx + 1, NGX), gy)
    before, after = (gx, wrap(gy - 1, NGY)), (gx, wrap(gy + 1, NGY))

    has_above = jnp.where(gx > 0, 1.0, 0.0).astype(f32)
    has_below = jnp.where(gx < NGX - 1, 1.0, 0.0).astype(f32)
    has_before = jnp.where(gy > 0, 1.0, 0.0).astype(f32)
    has_after = jnp.where(gy < NGY - 1, 1.0, 0.0).astype(f32)

    def merge_x(top, bottom):
        return jnp.where(iota(top.shape, 0) >= 4, top * has_above, bottom * has_below)

    def merge_y(left, right):
        return jnp.where(iota(left.shape, 0) >= 4, left * has_before, right * has_after)

    def send(src, dst, send_sem, recv_sem, device):
        pltpu.make_async_remote_copy(
            src_ref=src,
            dst_ref=dst,
            send_sem=send_sem,
            recv_sem=recv_sem,
            device_id=device,
            device_id_type=MESH,
        ).start()

    def arrive(ref, sem):
        pltpu.make_async_copy(ref, ref, sem).wait()

    loads = [
        pltpu.make_async_copy(src, dst, load_sem.at[i])
        for i, (src, dst) in enumerate(
            [
                (cot_in.at[0], surf),
                (cot_in.at[1], ebuf.at[0, z]),
                (cot_in.at[2], nbuf.at[0, nslot]),
                (traj_in, traj),
                (depth_in, depth),
                (line_in, line),
                (column_in, column),
                (owner_in, owner),
                (cell_in, cell),
                (obs_in, obs),
                (weight_in, weight),
            ]
        )
    ]

    barrier = pltpu.get_barrier_semaphore()
    peers = (
        [at_z(d) for d in reversed(RING)]
        + [(gx, lax.rem(gy + d, NGY)) for d in (8, 9, 7, 10, 6, 11, 5, 12, 4, 13, 3, 14, 2, 15, 1)]
        + [at_x(d) for d in reversed(XS)]
        + [above, below]
    )
    for copy in loads[0:3]:
        copy.start()
    for peer in peers:
        pl.semaphore_signal(barrier, inc=1, device_id=peer, device_id_type=MESH)
    for i in (5, 6, 3, 4, 7, 8, 9, 10):
        loads[i].start()
    part = NZ_CHIPS * ROWS

    def part_of(at):
        return pl.ds(pl.multiple_of(at * part, part), part)

    def pack_gauges():
        owners = owner[...]
        member = jnp.where(iota((NGY, COLS), 0) == owners, 1.0, 0.0).astype(f32)
        upper = jnp.where(iota((COLS, COLS), 0) <= iota((COLS, COLS), 1), 1.0, 0.0).astype(bf16)
        counted = dot(member.astype(bf16), upper)
        rank = jnp.sum(counted * member, axis=0, keepdims=True).astype(jnp.int32) - 1
        target = owners * 16 + rank
        picked = jnp.where(iota((2 * COLS, COLS), 0) == target, 1.0, 0.0).astype(bf16)
        onehot[...] = picked
        cells = cell[...]
        row = lax.shift_right_logical(cells, 7).astype(f32)
        col = lax.bitwise_and(cells, COLS - 1).astype(f32)
        payload = jnp.concatenate([obs[...], weight[...], row, col, jnp.ones_like(row)], axis=0)
        parts = jnp.concatenate([p.astype(f32) for p in split3(payload)], axis=0).astype(bf16)
        placed = dot_nt(parts, picked)
        placed = placed[0:8] + placed[8:16] + placed[16:24]
        mod = lax.rem(gy, 8)
        for d in range(NGY):
            half = placed[:, (d // 8) * COLS : (d // 8 + 1) * COLS]
            gout[d] = pltpu.roll(half, wrap(mod - d % 8, 8) * 16, 1)

    def split_once():
        high, low = split2(line[:, part_of(x)])
        ll[0, 0:ROWS] = high
        ll[0, ROWS : 2 * ROWS] = low
        for k in range(NGY):
            at = slice(k * COLS, (k + 1) * COLS)
            high, low = split2(column[:, at].T)
            ct[at, 0:COLS] = high
            ct[at, COLS : 2 * COLS] = low
        for t in range(STEPS):
            for p, piece in enumerate(split3(traj[t, 0])):
                fields3[pl.ds((p * STEPS + t) * ROWS, ROWS)] = piece

    def send_z(s, these):
        mine = ebuf.at[s, z]
        for i in these:
            send(mine, mine, e_send.at[s], e_recv.at[s, i], at_z(RING[i]))

    def send_rims(s):
        surface = surf[...]
        turned = jnp.concatenate([surface, ebuf[s, z]], axis=0).T
        yh_out[s, 0] = turned[0:8]
        yh_out[s, 1] = turned[COLS - 8 :]
        send(yh_out.at[s, 0], yh_in.at[s, 1], yh_send.at[s], yh_recv.at[s, 1], before)
        send(yh_out.at[s, 1], yh_in.at[s, 0], yh_send.at[s], yh_recv.at[s, 0], after)

    def send_x_rims(s):
        surface = surf[...]
        north = nbuf[s, nslot]
        xh_out[s, 0, 0] = surface[0:8]
        xh_out[s, 0, 1] = north[0:8]
        xh_out[s, 1, 0] = surface[ROWS - 8 :]
        xh_out[s, 1, 1] = north[ROWS - 8 :]
        send(xh_out.at[s, 0], xh_in.at[s, 1], xh_send.at[s], xh_recv.at[s, 1], above)
        send(xh_out.at[s, 1], xh_in.at[s, 0], xh_send.at[s], xh_recv.at[s, 0], below)

    def send_y(s):
        own = nbuf.at[s, nslot]
        for i in (4, 5, 6, 2, 3, 0, 1):
            send(own, own, n_send.at[s], n_yrecv.at[s, i], at_y(RING[i]))
        send(own, own, n_send.at[s], n_crecv.at[s], sibling)

    def start_once():
        for j, d in enumerate(XS):
            piece = line.at[:, part_of(wrap(x + d, NX_CHIPS))]
            send(piece, lpart.at[j], l_send.at[0], l_recv.at[0, j], at_x(d))
        for i in (3, 4, 6, 7, 8, 9, 10):
            loads[i].wait()
        send(column.at[pl.ds(0, 8)], crim.at[1], once_send.at[4], once_recv.at[7], before)
        send(column.at[pl.ds(COLS - 8, 8)], crim.at[0], once_send.at[4], once_recv.at[8], after)
        pack_gauges()
        gin[gy] = gout[gy]
        for d in range(1, NGY):
            peer = lax.rem(gy + d, NGY)
            send(gout.at[peer], gin.at[gy], once_send.at[2], once_recv.at[4], (gx, peer))
        both = pl.ds(1, 2)
        send(traj.at[:, both, pl.ds(0, 8)], tx_in.at[1], once_send.at[0], once_recv.at[0], above)
        send(
            traj.at[:, both, pl.ds(ROWS - 8, 8)],
            tx_in.at[0],
            once_send.at[0],
            once_recv.at[1],
            below,
        )
        for t in range(STEPS):
            turned = jnp.concatenate([traj[t, 1], traj[t, 2]], axis=0).T
            ty_out[0, t] = turned[0:8]
            ty_out[1, t] = turned[COLS - 8 :]
        send(ty_out.at[0], ty_in.at[1], once_send.at[1], once_recv.at[2], before)
        send(ty_out.at[1], ty_in.at[0], once_send.at[1], once_recv.at[3], after)

    def gauges():
        arrive(gin.at[pl.ds(0, NGY - 1)], once_recv.at[4])
        mod = lax.rem(gy, 8)
        lane8 = iota((8, COLS), 1)
        total = None
        for half in range(2):
            record = gin[half * 8]
            for k in range(1, 8):
                record = jnp.where(lax.shift_right_logical(lane8, 4) == k, gin[half * 8 + k], record)
            valid = record[7:8] > 0.5
            row = record[5:6].astype(jnp.int32)
            col = record[6:7].astype(jnp.int32)
            in_col = jnp.where((iota((COLS, COLS), 0) == col) & valid, 1.0, 0.0).astype(bf16)
            in_row = jnp.where(iota((ROWS, COLS), 0) == row, 1.0, 0.0).astype(f32)
            seen = dot(fields3[...], in_col)
            misfits, parts = [], [[], [], []]
            for t in range(STEPS):
                at = [seen[(p * STEPS + t) * ROWS : (p * STEPS + t + 1) * ROWS] for p in range(3)]
                value = jnp.sum((at[0] + at[1] + at[2]) * in_row, axis=0, keepdims=True)
                misfit = jnp.where(valid, value - record[t : t + 1], 0.0)
                misfits.append(misfit)
                for p, piece in enumerate(split3(record[4:5] * misfit)):
                    parts[p].append((in_row * piece.astype(f32)).astype(bf16))
            back = jnp.concatenate(misfits + [jnp.zeros((4, COLS), f32)], axis=0)
            for k in range(8):
                rout[half * 8 + k] = pltpu.roll(back, wrap(mod - k, 8) * 16, 1)
            spread = dot_nt(jnp.concatenate(parts[0] + parts[1] + parts[2], axis=0), in_col)
            total = spread if total is None else total + spread
        size = STEPS * ROWS
        total = total[0:size] + total[size : 2 * size] + total[2 * size :]
        for t in range(STEPS):
            forcing[t] = total[t * ROWS : (t + 1) * ROWS]
        rin[gy] = rout[gy]
        for d in range(1, NGY):
            peer = lax.rem(gy + d, NGY)
            send(rout.at[peer], rin.at[gy], once_send.at[5], once_recv.at[9], (gx, peer))

    def pass_rims():
        arrive(lrim.at[0], once_recv.at[5])
        arrive(lrim.at[0], once_recv.at[6])
        lmerged[...] = merge_x(lrim[0], lrim[1])
        for j, d in enumerate(XS):
            piece = lmerged.at[:, part_of(wrap(x + d, NX_CHIPS))]
            send(piece, lrimpart.at[j], l_send.at[1], l_recv.at[1, j], at_x(d))

    def both_parts(rim):
        high = rim.astype(bf16).astype(f32)
        return jnp.concatenate([high, rim - high], axis=0).astype(bf16)

    def prepare():
        for j in range(3):
            arrive(lpart.at[j], l_recv.at[0, j])
            high, low = split2(lpart[j])
            ll[1 + j, 0:ROWS] = high
            ll[1 + j, ROWS : 2 * ROWS] = low

    def prepare_rims():
        ll[0, 2 * ROWS :] = both_parts(lmerged[:, part_of(x)])
        for j in range(3):
            arrive(lrimpart.at[j], l_recv.at[1, j])
            ll[1 + j, 2 * ROWS :] = both_parts(lrimpart[j])

    def prepare_column():
        arrive(crim.at[0], once_recv.at[7])
        arrive(crim.at[0], once_recv.at[8])
        cx[...] = both_parts(merge_y(crim[0], crim[1]))

    def spread_y(merged):
        return jnp.concatenate([merged, jnp.zeros((COLS - 16, COLS), f32), merged], axis=0).T

    def rim_y(left, right):
        return spread_y(merge_y(left, right))

    def residuals():
        arrive(rin.at[pl.ds(0, NGY - 1)], once_recv.at[9])
        lane8 = iota((8, COLS), 1)
        halves = []
        for half in range(2):
            record = rin[half * 8]
            for k in range(1, 8):
                record = jnp.where(lax.shift_right_logical(lane8, 4) == k, rin[half * 8 + k], record)
            halves.append(record)
        returned = jnp.concatenate(halves, axis=1)
        pieces = jnp.concatenate([p.astype(f32) for p in split3(returned)], axis=0).astype(bf16)
        found = dot(pieces, onehot[...])
        residual_out[...] = found[0:4] + found[8:12] + found[16:20]

    def left_step(s):
        arrive(ebuf.at[s, pl.ds(0, NZ_CHIPS - 1)], e_send.at[s])
        arrive(pout.at[s], p_send.at[s])
        arrive(qout.at[s], q_send.at[s])
        arrive(nbuf.at[s, pl.ds(0, NGY - 1)], n_send.at[s])
        arrive(eedge.at[s, pl.ds(0, NZ_CHIPS - 1)], ee_send.at[s])
        arrive(nedge.at[s, pl.ds(0, NGY - 1)], ne_send.at[s])
        arrive(xh_out.at[s], xh_send.at[s])
        arrive(yh_out.at[s], yh_send.at[s])

    def left_once():
        arrive(lpart, l_send.at[0])
        arrive(lrimpart, l_send.at[1])
        arrive(tx_in, once_send.at[0])
        arrive(ty_out, once_send.at[1])
        arrive(gout.at[pl.ds(0, NGY - 1)], once_send.at[2])
        arrive(lrim, once_send.at[3])
        arrive(crim, once_send.at[4])
        arrive(rout.at[pl.ds(0, NGY - 1)], once_send.at[5])

    def step(s, carry):
        t = STEPS - 1 - s
        def keep(at, block):
            high, low = split2(block)
            rows = pl.ds(pl.multiple_of(at * ROWS, ROWS), ROWS)
            ez[rows, 0:COLS] = high
            ez[rows, COLS : 2 * COLS] = low

        def from_z(i):
            at = wrap(z - RING[i], NZ_CHIPS)
            arrive(ebuf.at[s, at], e_recv.at[s, i])
            keep(at, ebuf[s, at])

        def from_y(i):
            block = nbuf.at[s, core * NY_CHIPS + wrap(y - RING[i], NY_CHIPS)]
            arrive(block, n_yrecv.at[s, i])
            send(block, block, n_send.at[s], n_crecv.at[s], sibling)

        keep(z, ebuf[s, z])
        arrive(yh_in.at[s, 0], yh_recv.at[s, 0])
        arrive(yh_in.at[s, 0], yh_recv.at[s, 1])
        eedge[s, z] = merge_y(yh_in[s, 0], yh_in[s, 1])
        for d in RING:
            send(eedge.at[s, z], eedge.at[s, z], ee_send.at[s], ee_recv.at[s], at_z(d))
        arrive(xh_in.at[s, 0], xh_recv.at[s, 0])
        arrive(xh_in.at[s, 1], xh_recv.at[s, 1])
        nedge[s, nslot] = merge_x(xh_in[s, 0, 1], xh_in[s, 1, 1])
        for d in RING:
            send(nedge.at[s, nslot], nedge.at[s, nslot], ne_send.at[s], ne_recv.at[s, 0], at_y(d))

        @pl.when(s == 0)
        def _():
            pass_rims()

        from_y(0)
        from_y(1)
        from_z(0)
        from_z(1)
        from_y(2)
        from_y(3)
        from_z(2)
        from_z(3)

        @pl.when(s == 0)
        def _():
            split_once()

        from_z(4)
        from_z(5)
        from_z(6)

        @pl.when(s == 0)
        def _():
            prepare()

        def side_share(slot):
            return turned_rim(dot_nt(ae[...], ll[slot, 0 : 2 * ROWS, :]))

        def line_share(slot):
            return dot(ll[slot, 0 : 2 * ROWS], ez[...])

        def rim_share(slot):
            return dot(ll[slot, 2 * ROWS :], ez[...])

        def inner_of(product):
            left, right = product[:, 0:COLS], product[:, COLS:]
            return left[0:ROWS] + (right[0:ROWS] + left[ROWS : 2 * ROWS])

        def rim_of(product, at):
            left, right = product[:, 0:COLS], product[:, COLS:]
            return left[at : at + 8] + (right[at : at + 8] + left[at + 8 : at + 16])

        def turned_rim(product):
            return product[0:8] + (pltpu.roll(product[0:8], ROWS, 1) + product[8:16])

        for j in (2, 0, 1):
            pout[s, j] = inner_of(line_share(1 + j))
            send(pout.at[s, j], pin.at[s, j], p_send.at[s], p_recv.at[s, j], at_x(-XS[j]))

        @pl.when(s == 0)
        def _():
            prepare_rims()

        for j in (2, 0, 1):
            qout[s, j, 0:8] = rim_of(rim_share(1 + j), 0)
        line_adjoint = inner_of(line_share(0))
        line_x = rim_of(rim_share(0), 0)
        arrive(eedge.at[s, pl.ds(0, NZ_CHIPS - 1)], ee_recv.at[s])
        lane = iota((8, COLS), 1)
        for k in range(NZ_CHIPS // 2):
            rim = jnp.where(lane < ROWS, pltpu.roll(eedge[s, 2 * k], ROWS, 1), eedge[s, 2 * k + 1])
            ae[:, k * COLS : (k + 1) * COLS] = both_parts(rim)
        for j in (2, 0, 1):
            qout[s, j, 8:16] = side_share(1 + j)
            send(qout.at[s, j], qin.at[s, j], q_send.at[s], q_recv.at[s, j], at_x(-XS[j]))
        from_y(4)
        from_y(5)
        from_y(6)
        arrive(nedge.at[s, pl.ds(0, NY_CHIPS - 1)], ne_recv.at[s, 0])
        column_edges = nedge.at[s, pl.ds(core * NY_CHIPS, NY_CHIPS)]
        send(column_edges, column_edges, ne_send.at[s], ne_recv.at[s, 1], sibling)
        line_y = side_share(0)

        @pl.when(s == 0)
        def _():
            arrive(tx_in.at[0], once_recv.at[0])
            arrive(tx_in.at[0], once_recv.at[1])
            arrive(ty_in.at[0], once_recv.at[2])
            arrive(ty_in.at[0], once_recv.at[3])
            prepare_column()
            gauges()

        surface = surf[...]
        east, north = traj[t, 1], traj[t, 2]
        whole = depth[...] + traj[t, 0]
        rim_surface = rim_y(yh_in[s, 0], yh_in[s, 1])[0:ROWS]
        flux_x = mass_rate * slope_x(surface, merge_x(xh_in[s, 0, 0], xh_in[s, 1, 0]))
        flux_y = mass_rate * slope_y(surface, rim_surface)
        gain = east * flux_x + north * flux_y
        depth_out[...] = jnp.where(s == 0, 0.0, depth_out[...]) + gain
        base[0] = surface + gain
        base[1] = whole * flux_x
        base[2] = whole * flux_y
        rims = rim_y(ty_in[0, t], ty_in[1, t])
        east_x = merge_x(tx_in[0, t, 0], tx_in[1, t, 0])
        north_x = merge_x(tx_in[0, t, 1], tx_in[1, t, 1])
        north_y = rims[ROWS:]
        coef[0] = 1.0 - advect_rate * slope_x(east, east_x)
        coef[1] = advect_rate * slope_x(north, north_x)
        coef[2] = advect_rate * slope_y(east, rims[0:ROWS])
        coef[3] = 1.0 - advect_rate * slope_y(north, north_y)

        arrive(nbuf.at[s, pl.ds(0, NY_CHIPS)], n_crecv.at[s])
        arrive(nedge.at[s, pl.ds(0, NY_CHIPS)], ne_recv.at[s, 1])
        for k in range(NGY):
            at = ((k % NY_CHIPS) * 2 + k // NY_CHIPS) * COLS
            at = slice(at, at + COLS)
            high, low = split2(nbuf[s, k])
            nn[0:ROWS, at] = high
            nn[ROWS : 2 * ROWS, at] = low
            nn[2 * ROWS : 2 * ROWS + 16, at] = both_parts(nedge[s, k])
        product = dot(nn[...], ct[...])
        column_adjoint, column_x = inner_of(product), rim_of(product, 2 * ROWS)
        column_y = spread_y(turned_rim(dot_nt(cx[...], nn[0 : 2 * ROWS, :])))[0:ROWS]

        @pl.when(s > 0)
        def _():
            left_step(s - 1)

        @pl.when(s == 2)
        def _():
            residuals()
            left_once()

        for j in range(3):
            arrive(qin.at[s, j], q_recv.at[s, j])
            line_x += qin[s, j, 0:8]
            line_y += qin[s, j, 8:16]
        line_y = spread_y(line_y)[0:ROWS]
        for j in range(3):
            arrive(pin.at[s, j], p_recv.at[s, j])
            line_adjoint += pin[s, j]

        along_x = slope_x(line_adjoint, line_x)
        along_y = slope_y(column_adjoint, column_y)
        mixed = slope_x(east * line_adjoint, east_x * line_x) + slope_y(
            north * line_adjoint, north_y * line_y
        )
        ebuf[s + 1, z] = (
            line_adjoint * coef[0] - column_adjoint * coef[1] + advect_rate * mixed + base[1]
        )

        surf[...] = base[0] + forcing[t] + slope_rate * (along_x + along_y)
        mixed = slope_x(east * column_adjoint, east_x * column_x) + slope_y(
            north * column_adjoint, north_y * column_y
        )
        nbuf[s + 1, nslot] = (
            column_adjoint * coef[3] - line_adjoint * coef[2] + advect_rate * mixed + base[2]
        )

        @pl.when(s < STEPS - 1)
        def _():
            send_x_rims(s + 1)
            send_z(s + 1, (6, 4, 5, 0, 1, 2, 3))
            send_rims(s + 1)
            send_y(s + 1)

        return carry

    for i in range(3):
        loads[i].wait()
    pl.semaphore_wait(barrier, len(peers))
    send_x_rims(0)
    loads[5].wait()
    send(line.at[pl.ds(0, 8)], lrim.at[1], once_send.at[3], once_recv.at[5], above)
    send(line.at[pl.ds(ROWS - 8, 8)], lrim.at[0], once_send.at[3], once_recv.at[6], below)
    send_z(0, (6, 4, 5, 0, 1, 2, 3))
    send_rims(0)
    send_y(0)
    start_once()
    lax.fori_loop(0, STEPS, step, 0)

    state_out[0] = surf[...]
    state_out[1] = ebuf[STEPS, z]
    state_out[2] = nbuf[STEPS, nslot]

    left_step(STEPS - 1)


def hand_over(state_in, depth_in, residual_in, state_out, depth_out, residual_out):
    state_out[...] = state_in[...]
    depth_out[...] = depth_in[...]
    residual_out[...] = residual_in[...]


def per_device(
    trajectory,
    depth,
    cotangent,
    line_inverse,
    column_inverse,
    gauge_owner,
    gauge_cell,
    gauge_obs,
    gauge_weight,
):
    vmem = pltpu.VMEM
    dma = pltpu.SemaphoreType.DMA
    scratch = [
        vmem((STEPS, 3, ROWS, COLS), f32),
        vmem((ROWS, COLS), f32),
        vmem((ROWS, 2048), f32),
        vmem((COLS, 2048), f32),
        vmem((1, COLS), jnp.int32),
        vmem((1, COLS), jnp.int32),
        vmem((STEPS, COLS), f32),
        vmem((1, COLS), f32),
        vmem((ROWS, COLS), f32),
        vmem((STEPS + 1, NZ_CHIPS, ROWS, COLS), f32),
        vmem((STEPS + 1, NGY, ROWS, COLS), f32),
        vmem((STEPS, NZ_CHIPS, 8, COLS), f32),
        vmem((STEPS, NGY, 8, COLS), f32),
        vmem((STEPS, 2, 2, 8, COLS), f32),
        vmem((STEPS, 2, 2, 8, COLS), f32),
        vmem((STEPS, 2, 8, COLS), f32),
        vmem((STEPS, 2, 8, COLS), f32),
        vmem((2, 8, 2048), f32),
        vmem((2, 8, 2048), f32),
        vmem((2, STEPS, 2, 8, COLS), f32),
        vmem((2, STEPS, 8, COLS), f32),
        vmem((2, STEPS, 8, COLS), f32),
        vmem((NGY, 8, COLS), f32),
        vmem((NGY, 8, COLS), f32),
        vmem((NGY, 8, COLS), f32),
        vmem((NGY, 8, COLS), f32),
        vmem((3, ROWS, 512), f32),
        vmem((3, 8, 512), f32),
        vmem((8, 2048), f32),
        vmem((STEPS, 3, ROWS, COLS), f32),
        vmem((STEPS, 3, ROWS, COLS), f32),
        vmem((STEPS, 3, 16, COLS), f32),
        vmem((STEPS, 3, 16, COLS), f32),
        vmem((2 * COLS, COLS), bf16),
        vmem((4, 2 * ROWS + 16, 512), bf16),
        vmem((2048, 2 * COLS), bf16),
        vmem((16, 2048), bf16),
        vmem((2 * ROWS + 16, 2048), bf16),
        vmem((16, 512), bf16),
        vmem((512, 2 * COLS), bf16),
        vmem((3 * STEPS * ROWS, COLS), bf16),
        vmem((STEPS, ROWS, COLS), f32),
        vmem((3, ROWS, COLS), f32),
        vmem((4, ROWS, COLS), f32),
        dma((11,)),
        dma((STEPS,)),
        dma((STEPS, 7)),
        dma((STEPS,)),
        dma((STEPS, 3)),
        dma((STEPS,)),
        dma((STEPS, 3)),
        dma((STEPS,)),
        dma((STEPS, 7)),
        dma((STEPS,)),
        dma((STEPS,)),
        dma((STEPS,)),
        dma((STEPS,)),
        dma((STEPS, 2)),
        dma((STEPS,)),
        dma((STEPS, 2)),
        dma((STEPS,)),
        dma((STEPS, 2)),
        dma((2,)),
        dma((2, 3)),
        dma((6,)),
        dma((10,)),
    ]
    anywhere = pl.BlockSpec(memory_space=pl.ANY)
    here = pl.BlockSpec(memory_space=pltpu.VMEM)
    results = pl.pallas_call(
        kernel,
        name="adjoint",
        out_shape=(
            jax.ShapeDtypeStruct((3, ROWS, COLS), f32),
            jax.ShapeDtypeStruct((ROWS, COLS), f32),
            jax.ShapeDtypeStruct((STEPS, COLS), f32),
        ),
        in_specs=[anywhere] * 9,
        out_specs=(here, here, here),
        scratch_shapes=scratch,
        compiler_params=pltpu.CompilerParams(
            collective_id=0, has_side_effects=True, vmem_limit_bytes=60 * 2**20
        ),
    )(
        trajectory,
        depth,
        cotangent,
        line_inverse,
        column_inverse,
        gauge_owner.reshape(1, COLS),
        gauge_cell.reshape(1, COLS),
        gauge_obs,
        gauge_weight.reshape(1, COLS),
    )
    return pl.pallas_call(
        hand_over,
        name="hand_over",
        out_shape=tuple(jax.ShapeDtypeStruct(r.shape, r.dtype) for r in results),
        in_specs=[here] * 3,
        out_specs=(here, here, here),
    )(*results)


def solution(mesh):
    return jax.shard_map(
        per_device,
        mesh=mesh,
        in_specs=(
            P(None, None, "gx", "gy"),
            P("gx", "gy"),
            P(None, "gx", "gy"),
            P("gx", None),
            P("gy", None),
            P(("gx", "gy"), None),
            P(("gx", "gy")),
            P(None, ("gx", "gy")),
            P(("gx", "gy")),
        ),
        out_specs=(P(None, "gx", "gy"), P("gx", "gy"), P(None, ("gx", "gy"))),
        check_vma=False,
    )
```
